128 devices in a mesh: gx: 32 (over x, y, core), gy: 4 (over z).
Axes of the slice: x: 4, y: 4, z: 4, core: 2. Of those that a mesh axis runs over, the one named last changes fastest.
Arguments:
- right_side: float32 [1024, 512, 128], P('gx', 'gy'), may hold values from -8 to 8
- sea_mask: int32 [1024, 512], P('gx', 'gy'), may hold values 0 or 1
- vertical_coupling: float32 [127], replicated, may hold values from 1 to 16
Outputs:
- solution_field: float32 [1024, 512, 128], P('gx', 'gy')
- residual: float32 [1024, 512, 128], P('gx', 'gy')
The draws below stay inside these ranges and needn't reach their ends.
All inputs are finite; a program needn't handle non-finite values. No bound on the sum of `sea_mask` on one device may be relied on, other than what follows from the above.
Results may differ from the reference program's by a relative error of at most 0.0003.
Values sent between devices are 32-bit elements; how exact they have to be, the bound alone decides.
A program may use at most 128 MiB of HBM per device.

```python
import math
import jax
import jax.numpy as jnp
from jax import lax

NZ = 128
ITERS = 3
SWEEPS = 4
NX = 1024
NY = 512


def set_ends(array, stream_key, smallest, high):
    longest = array.shape.index(max(array.shape))
    spots = []
    for shift in (0, 1):
        where = [jax.random.randint(jax.random.fold_in(stream_key, axis), (), 0, length) for axis, length in enumerate(array.shape)]
        where[longest] = (where[longest] + shift) % array.shape[longest]
        spots.append(tuple(where))
    return array.at[spots[0]].set(smallest).at[spots[1]].set(high)


def block_scale(stream_key, dims, pieces, least, top_value):
    def one(dim, blocks):
        steps = jax.random.uniform(jax.random.fold_in(jax.random.fold_in(stream_key, 6), dim), (blocks,), jnp.float32, least / len(pieces), top_value / len(pieces))
        return jnp.repeat(jnp.exp(steps), dims[dim] // blocks).reshape((-1,) + (1,) * (len(dims) - dim - 1))

    gain = one(*pieces[0])
    for cut in pieces[1:]:
        gain = gain * one(*cut)
    return gain


def bell_draw(key, shape, width, bound, split=(), kind=jnp.bfloat16):
    entries = jax.random.normal(key, shape, jnp.float32) * width
    if len(split) > 0:
        entries = block_scale(key, shape, split, -0.22, 0.18) * entries
    return jnp.clip(entries, min=-bound, max=bound).astype(kind)


def setup_inputs(seed: int = 0) -> dict:
    arg_keys = jax.random.split(jax.random.key(seed), 4)
    right_side = bell_draw(arg_keys[0], (NX, NY, NZ), 1.0, 8.0, ((0, 32), (1, 4)), jnp.float32)
    sea_mask = set_ends((jax.random.randint(arg_keys[1], (NX, NY), 0, 10) < 9).astype(jnp.int32), jax.random.fold_in(arg_keys[1], 1), 0, 1)
    vertical_coupling = jnp.clip(jnp.exp(jax.random.uniform(arg_keys[2], (NZ - 1,), jnp.float32, math.log(1.0), math.log(16.0))), 1.0, 16.0)
    return dict(right_side=right_side, sea_mask=sea_mask, vertical_coupling=vertical_coupling)


shift_term = 0.1
coarse_diag = 4.4
damping = 0.8

def line_inverse(coupling, diag_value, factor):
    count = coupling.shape[0] + 1
    upper = jnp.pad(coupling, (0, 1))
    lower = jnp.pad(coupling, (1, 0))
    matrix = factor * (jnp.diag(upper + lower) - jnp.diag(coupling, 1) - jnp.diag(coupling, -1))
    matrix = matrix + diag_value * jnp.eye(count, dtype=matrix.dtype)
    chol = jnp.linalg.cholesky(matrix)
    return jax.scipy.linalg.cho_solve((chol, True), jnp.eye(count, dtype=matrix.dtype))

def line_apply(field, inverse):
    shape = field.shape
    flat = jnp.dot(field.reshape(-1, shape[-1]), inverse, precision=lax.Precision.HIGHEST)
    return flat.reshape(shape)

def line_smooth(field, maskf, inverse):
    return maskf[..., None] * line_apply(field, inverse) + (1.0 - maskf[..., None]) * field

def operate_padded(padded, mask_pad, coupling):
    value = padded[1:-1, 1:-1]
    maskf = mask_pad[1:-1, 1:-1]
    horiz = mask_pad[2:, 1:-1, None] * (value - padded[2:, 1:-1])
    horiz = horiz + mask_pad[:-2, 1:-1, None] * (value - padded[:-2, 1:-1])
    horiz = horiz + mask_pad[1:-1, 2:, None] * (value - padded[1:-1, 2:])
    horiz = horiz + mask_pad[1:-1, :-2, None] * (value - padded[1:-1, :-2])
    flux = coupling * (value[..., :-1] - value[..., 1:])
    vertical = jnp.pad(flux, ((0, 0), (0, 0), (0, 1))) - jnp.pad(flux, ((0, 0), (0, 0), (1, 0)))
    inner = shift_term * value + vertical + horiz
    return maskf[..., None] * inner + (1.0 - maskf[..., None]) * value

def coarse_sweep(padded, target):
    value = padded[1:-1, 1:-1]
    beside = padded[2:, 1:-1] + padded[:-2, 1:-1] + padded[1:-1, 2:] + padded[1:-1, :-2]
    applied = coarse_diag * value - beside
    return value + damping * (target - applied) / coarse_diag

def reference(right_side, sea_mask, vertical_coupling):
    maskf = sea_mask.astype(jnp.float32)
    mask_pad = jnp.pad(maskf, 1)
    inv_fine = line_inverse(vertical_coupling, 4.1, 1.0)
    inv_coarse = line_inverse(vertical_coupling, 4.4, 4.0)

    def operate(field):
        return operate_padded(jnp.pad(field, ((1, 1), (1, 1), (0, 0))), mask_pad, vertical_coupling)

    def precondition(source):
        first = line_smooth(source, maskf, inv_fine)
        left = source - operate(first)
        nx, ny, nz = left.shape
        coarse = left.reshape(nx // 2, 2, ny // 2, 2, nz).sum(axis=(1, 3))
        corr = line_apply(coarse, inv_coarse)
        target = jnp.sum(coarse, axis=2) / nz
        level = jnp.zeros_like(target)
        for sweep in range(SWEEPS):
            level = coarse_sweep(jnp.pad(level, 1), target)
        corr = corr + level[..., None]
        fine = jnp.repeat(jnp.repeat(corr, 2, axis=0), 2, axis=1)
        guess = first + maskf[..., None] * fine
        return guess + line_smooth(source - operate(guess), maskf, inv_fine)
    solution_field = jnp.zeros_like(right_side)
    residual = right_side
    u_vec = precondition(residual)
    w_vec = operate(u_vec)
    z_vec = q_vec = s_vec = p_vec = jnp.zeros_like(right_side)
    gamma_prev = jnp.float32(1.0)
    alpha_prev = jnp.float32(1.0)
    for step in range(ITERS):
        gamma = jnp.sum(residual * u_vec)
        delta = jnp.sum(w_vec * u_vec)
        m_vec = precondition(w_vec)
        n_vec = operate(m_vec)
        if step == 0:
            beta = jnp.zeros_like(gamma)
            alpha = gamma / delta
        else:
            beta = gamma / gamma_prev
            alpha = gamma / (delta - beta * gamma / alpha_prev)
        z_vec = n_vec + beta * z_vec
        q_vec = m_vec + beta * q_vec
        s_vec = w_vec + beta * s_vec
        p_vec = u_vec + beta * p_vec
        solution_field = solution_field + alpha * p_vec
        residual = residual - alpha * s_vec
        u_vec = u_vec - alpha * q_vec
        w_vec = w_vec - alpha * z_vec
        gamma_prev = gamma
        alpha_prev = alpha
    return (solution_field, residual)
```

```python
import functools

import jax
import jax.numpy as jnp
from jax import lax
from jax.experimental import pallas as pl
from jax.experimental.pallas import tpu as pltpu
from jax.sharding import PartitionSpec as P


ITERS = 3
SWEEPS = 4
F32 = jnp.float32
BF16 = jnp.bfloat16
MESH = pl.DeviceIdType.MESH
NXL, NY2, NZ = 32, 64, 128
ROWS = 8
SIDES = [(dx, dy) for dx in (-1, 0, 1) for dy in (-1, 0, 1) if (dx, dy) != (0, 0)]


def split_mm(v, w):
    high = v.astype(BF16)
    low = (v - high.astype(F32)).astype(BF16)
    o = jnp.dot(jnp.concatenate([high, low], axis=1), w, preferred_element_type=F32)
    return o[:, :128] + o[:, 128:]


def roll(v, shift, axis):
    return pltpu.roll(v, shift % v.shape[axis], axis)


def line_inverses(coupling, w_refs):
    lane = lax.broadcasted_iota(jnp.int32, (8, 128), 1)
    row = lax.broadcasted_iota(jnp.int32, (8, 128), 0)
    up = jnp.broadcast_to(coupling, (8, 128))
    lo = roll(up, 1, 1)
    factor = jnp.where(row == 0, 1.0, 4.0)
    diag = jnp.where(row == 0, 4.1, 4.4) + factor * (up + lo)
    off_up = factor * up
    off_lo = factor * lo

    def pivots(off, step):
        a, b = diag, -off * off
        c, d = jnp.ones_like(a), jnp.zeros_like(a)
        s = 1
        while s < 128:
            inside = (lane >= s) if step > 0 else (lane < 128 - s)
            ra = jnp.where(inside, roll(a, step * s, 1), 1.0)
            rb = jnp.where(inside, roll(b, step * s, 1), 0.0)
            rc = jnp.where(inside, roll(c, step * s, 1), 0.0)
            rd = jnp.where(inside, roll(d, step * s, 1), 1.0)
            na, nb = a * ra + b * rc, a * rb + b * rd
            nc, nd = c * ra + d * rc, c * rb + d * rd
            inv = 1.0 / na
            a, b, c, d = jnp.ones_like(a), nb * inv, nc * inv, nd * inv
            s *= 2
        return 1.0 / c

    fore = pivots(off_lo, 1)
    back = pivots(off_up, -1)
    main = 1.0 / (fore + back - diag)
    ratio = jnp.where(lane < 127, jnp.log(jnp.maximum(off_up, 1e-30) / fore), 0.0)
    total = jnp.where(lane >= 1, roll(ratio, 1, 1), 0.0)
    s = 1
    while s < 128:
        total = total + jnp.where(lane >= s, roll(total, s, 1), 0.0)
        s *= 2

    r = lax.broadcasted_iota(jnp.int32, (128, 128), 0)
    c = lax.broadcasted_iota(jnp.int32, (128, 128), 1)
    for i, w_ref in enumerate(w_refs):
        def wide(v):
            return jnp.broadcast_to(v[i : i + 1], (128, 128))

        g_row, t_row = wide(main), wide(total)
        g_col, t_col = g_row.T, t_row.T
        g = jnp.where(r <= c, g_row, g_col) * jnp.exp(-jnp.abs(t_row - t_col))
        a_col, u_col = wide(diag).T, wide(off_up).T
        l_col = wide(off_lo).T
        tg = a_col * g - u_col * roll(g, -1, 0) - l_col * roll(g, 1, 0)
        rest = jnp.where(r == c, 1.0, 0.0) - tg
        g = g + jnp.dot(g.astype(BF16), rest.astype(BF16), preferred_element_type=F32)
        high = g.astype(BF16)
        low = (g - high.astype(F32)).astype(BF16)
        both = jnp.concatenate([high, low], axis=1)
        w_ref[...] = jnp.concatenate([both, both], axis=0)


def kernel(
    nx, ny, rhs_ref, mask_ref, coup_ref, x_ref, r_ref,
    inp, outx, outr, fb, ys, rhos, m3, q3, t1s, h1s, hy, sy, w0, w1, kpad,
    blk, nbr, tmat, mn, m2, bars, ybars, nus, red1, red2,
    in_sem, out_sem, sx_sem, rx_sem, sb_sem, rb_sem, s1_sem, r1_sem, s2_sem, r2_sem,
):
    gx, gy = lax.axis_index("gx"), lax.axis_index("gy")
    lo, hi = lax.rem(gx, 4), lax.div(gx, 4)
    ng = nx // 4

    first = [(dl, dg) for dl in range(4) for dg in range(ny) if (dl, dg) != (0, 0)]
    second = list(range(1, ng))

    def first_dev(dl, dg):
        return (hi * 4 + lax.rem(lo + dl, 4), lax.rem(gy + dg, ny))

    def second_dev(dh):
        return (lax.rem(hi + dh, ng) * 4 + lo, gy)

    def side_dev(dx, dy):
        return (lax.rem(gx + dx + nx, nx), lax.rem(gy + dy + ny, ny))

    load = pltpu.make_async_copy(rhs_ref, inp, in_sem)
    load.start()

    def clear(k, carry):
        zero = jnp.zeros((NY2, 128), F32)
        for b in range(2):
            fb[k, 0, b, 8:72, :] = zero
            fb[k, NXL + 1, b, 8:72, :] = zero
        hy[k] = jnp.zeros((2, NXL, 128), F32)
        return carry

    lax.fori_loop(0, 3 * ITERS, clear, 0)
    nbr[...] = jnp.zeros(nbr.shape, F32)

    barrier = pltpu.get_barrier_semaphore()
    for dx, dy in SIDES:
        pl.semaphore_signal(barrier, inc=1, device_id=side_dev(dx, dy), device_id_type=MESH)
    for dl, dg in first:
        pl.semaphore_signal(barrier, inc=1, device_id=first_dev(dl, dg), device_id_type=MESH)
    for dh in second:
        pl.semaphore_signal(barrier, inc=1, device_id=second_dev(dh), device_id_type=MESH)

    kpad[...] = jnp.zeros((1, 128), F32)
    kpad[:, 0:127] = coup_ref[...]
    line_inverses(kpad[...], (w0, w1))

    lane = lax.broadcasted_iota(jnp.int32, (NY2, 128), 1)

    def to_columns(v):
        tmat[...] = jnp.concatenate([v, jnp.zeros((128 - NXL, 128), F32)], axis=0).T

    def expand(dst):
        for b in range(2):
            col = tmat[pl.ds(b, NY2, stride=2), :]
            for x in range(NXL):
                dst[x, b] = jnp.broadcast_to(col[:, x : x + 1], (NY2, 128))

    mask = mask_ref[...].astype(F32)
    blk[0:NXL, :] = mask
    to_columns(mask)
    expand(m3)

    load.wait()

    def start_pass(x, carry):
        acc, means = carry[0], list(carry[1:])
        for b in range(2):
            v = inp[x, pl.ds(b, NY2, stride=2), :]
            m = m3[x, b]
            mean = jnp.sum(v, axis=1, keepdims=True) * (1.0 / NZ)
            means[b] = jnp.where(lane == x, mean, means[b])
            rhos[0, x, b] = m * (v - mean)
            land = (1.0 - m) * v
            acc = acc + jnp.sum((land * land).reshape(8, 8, 128), axis=0)
        return (acc, *means)

    zero = jnp.zeros((NY2, 128), F32)
    nu0, mean0, mean1 = lax.fori_loop(0, NXL, start_pass, (jnp.zeros((8, 128), F32), zero, zero))
    tmat[pl.ds(0, NY2, stride=2), :] = mean0
    tmat[pl.ds(1, NY2, stride=2), :] = mean1
    blk[NXL : 2 * NXL, :] = mask * tmat[...].T[0:NXL]

    pl.semaphore_wait(barrier, len(SIDES) + len(first) + len(second))

    def exists(dx, dy):
        ok = None
        for pos, d, n in ((gx, dx, nx), (gy, dy, ny)):
            if d:
                here = (pos + d >= 0) & (pos + d < n)
                ok = here if ok is None else ok & here
        return ok

    def block_copy(i):
        dx, dy = SIDES[i]
        return pltpu.make_async_remote_copy(
            src_ref=blk, dst_ref=nbr.at[i], send_sem=sb_sem.at[i], recv_sem=rb_sem.at[i],
            device_id=side_dev(dx, dy), device_id_type=MESH,
        )

    for i in range(8):
        pl.when(exists(*SIDES[i]))(lambda i=i: block_copy(i).start())

    def faces(k):
        field = fb.at[k]
        cells = pl.ds(8, NY2)
        ends = (
            (field.at[1, :, cells, :], field.at[NXL + 1, :, cells, :], (-1, 0)),
            (field.at[NXL, :, cells, :], field.at[0, :, cells, :], (1, 0)),
            (sy.at[k, 0], hy.at[k, 1], (0, -1)),
            (sy.at[k, 1], hy.at[k, 0], (0, 1)),
        )
        return [
            (
                pltpu.make_async_remote_copy(
                    src_ref=src, dst_ref=dst, send_sem=sx_sem.at[k, i], recv_sem=rx_sem.at[k, i],
                    device_id=side_dev(*d), device_id_type=MESH,
                ),
                exists(*d), exists(-d[0], -d[1]),
            )
            for i, (src, dst, d) in enumerate(ends)
        ]

    def send(k):
        for copy, there, _ in faces(k):
            pl.when(there)(copy.start)

    def receive(k):
        for copy, there, back in faces(k):
            pl.when(back)(copy.wait_recv)

    def put(k, x, b, v):
        fb[k, x + 1, b, 8:72, :] = v
        if b == 0:
            sy[k, 0, pl.ds(x, 1), :] = v[0:1]
        else:
            sy[k, 1, pl.ds(x, 1), :] = v[NY2 - 1 : NY2]

    def insert(k, x):
        fb[k, x + 1, 1, 7:8, :] = hy[k, 0, pl.ds(x, 1), :]
        fb[k, x + 1, 0, 72:73, :] = hy[k, 1, pl.ds(x, 1), :]

    def stencil(k, x, b):
        mate = fb[k, x + 1, 1 - b, 8:72, :]
        side = fb[k, x + 1, 1 - b, 7:71, :] if b == 0 else fb[k, x + 1, 1 - b, 9:73, :]
        beside = (fb[k, x, b, 8:72, :] + fb[k, x + 2, b, 8:72, :]) + (mate + side)
        return q3[x, b] * fb[k, x + 1, b, 8:72, :], beside

    def tile_sum(v):
        return jnp.sum(v.reshape(8, 8, 128), axis=0)

    def smooth0_pass(i, carry):
        for x8 in range(ROWS):
            x = i * ROWS + x8
            e0 = split_mm(rhos[0, x].reshape(128, 128), w0[...])
            put(0, x, 0, e0[:NY2])
            put(0, x, 1, e0[NY2:])
        return carry

    lax.fori_loop(0, NXL // ROWS, smooth0_pass, 0)
    send(0)

    for i in range(8):
        dx, dy = SIDES[i]
        pl.when(exists(-dx, -dy))(lambda i=i: block_copy(i).wait_recv())

    low_half = lax.broadcasted_iota(jnp.int32, (96, 128), 1) < 64

    def around(rows):
        def column(dy):
            parts = []
            for dx in (-1, 0, 1):
                if (dx, dy) == (0, 0):
                    parts.append(blk[rows, :])
                else:
                    parts.append(nbr[SIDES.index((-dx, -dy)), rows, :])
            return roll(jnp.concatenate(parts, axis=0), 64, 1)

        left, mid, right = column(-1), column(0), column(1)
        return jnp.concatenate(
            [jnp.where(low_half, left, mid), jnp.where(low_half, mid, right)], axis=1
        )

    def local(v):
        a, b = roll(v[32:64, 0:128], 64, 1), roll(v[32:64, 128:256], 64, 1)
        return jnp.where(low_half[:NXL], a, b)

    moves = ((-1, 0), (1, 0), (-1, 1), (1, 1))
    mask2 = around(pl.ds(0, NXL))
    m2[...] = mask2
    bars[0] = around(pl.ds(NXL, NXL))
    open_sides = jnp.zeros((96, 256), F32)
    for i, (s, axis) in enumerate(moves):
        beside = roll(mask2, s, axis)
        mn[i] = beside
        open_sides = open_sides + beside
    to_columns(local(mask2 * (4.0 - open_sides)))
    expand(q3)

    xi = lax.broadcasted_iota(jnp.int32, (96, 256), 0) + (gx * NXL - 32)
    yi = lax.broadcasted_iota(jnp.int32, (96, 256), 1) + (gy * 128 - 64)
    inside = (xi >= 0) & (xi < nx * NXL) & (yi >= 0) & (yi < ny * 128)
    dom = jnp.where(inside, 1.0, 0.0)

    even_x = lax.rem(lax.broadcasted_iota(jnp.int32, (96, 256), 0), 2) == 0
    even_y = lax.rem(lax.broadcasted_iota(jnp.int32, (96, 256), 1), 2) == 0

    def flow(v):
        total = None
        for i, (s, axis) in enumerate(moves):
            term = mn[i] * (roll(v, s, axis) - v)
            total = term if total is None else total + term
        return total

    def mean_step(j):
        m = m2[...]
        e0 = bars[j] * (1.0 / 4.1)
        t = 4.0 * e0 + flow(e0)
        t1 = m * t
        t1 = t1 + jnp.where(even_x, roll(t1, -1, 0), roll(t1, 1, 0))
        t1 = t1 + jnp.where(even_y, roll(t1, -1, 1), roll(t1, 1, 1))
        e1 = t1 * (1.0 / 4.4)
        c = (0.8 / 4.4) * t1
        for _ in range(SWEEPS - 1):
            beside = (roll(c, 2, 0) + roll(c, -2, 0)) + (roll(c, 2, 1) + roll(c, -2, 1))
            c = dom * (c + 0.8 * (t1 - (4.4 * c - beside)) / 4.4)
        f = e1 + c
        rem = m * (t + flow(f) + (e1 - 0.25 * t1) - 0.1 * c)
        d = rem * (1.0 / 4.1)
        ybars[j] = e0 + m * f + d
        bars[j + 1] = m * (4.0 * d + flow(d))

    def coarse_pass(k):
        def body(x2, carry):
            total = None
            for x in (2 * x2, 2 * x2 + 1):
                insert(k, x)
                for b in range(2):
                    own, beside = stencil(k, x, b)
                    t = own + m3[x, b] * beside
                    total = t if total is None else total + t
            t1s[x2] = total
            return carry

        lax.fori_loop(0, NXL // 2, body, 0)

    def correct_pass(k):
        def body(i, carry):
            t1 = t1s[pl.ds(i * 4, 4)].reshape(4 * NY2, 128)
            e1 = split_mm(t1, w1[...])
            h1s[pl.ds(i * 4, 4)] = (0.25 * t1 + 3.0 * e1).reshape(4, NY2, 128)
            for x8 in range(8):
                x = i * 8 + x8
                part = e1[(x8 // 2) * NY2 : (x8 // 2 + 1) * NY2]
                for b in range(2):
                    put(k + 1, x, b, fb[k, x + 1, b, 8:72, :] + m3[x, b] * part)
            return carry

        lax.fori_loop(0, NXL // 8, body, 0)

    def smooth_pass(k, j):
        def body(i, acc):
            for x8 in range(ROWS):
                x = i * ROWS + x8
                insert(k, x)
                rem = []
                for b in range(2):
                    own, beside = stencil(k, x, b)
                    rem.append(own + m3[x, b] * (beside - h1s[lax.div(x, 2)]))
                d = split_mm(jnp.concatenate(rem, axis=0), w0[...])
                for b in range(2):
                    part = d[b * NY2 : (b + 1) * NY2]
                    y = fb[k, x + 1, b, 8:72, :] + part
                    put(k + 1, x, b, part)
                    ys[j, x, b] = y
                    acc = acc + tile_sum(rhos[j, x, b] * y)
            return acc

        return lax.fori_loop(0, NXL // ROWS, body, jnp.zeros((8, 128), F32))

    def next_pass(k, j):
        def body(i, acc):
            for x8 in range(ROWS):
                x = i * ROWS + x8
                insert(k, x)
                new = []
                for b in range(2):
                    own, beside = stencil(k, x, b)
                    v = own + m3[x, b] * beside
                    rhos[j + 1, x, b] = v
                    acc = acc + tile_sum(v * ys[j, x, b])
                    new.append(v)
                if j + 1 < ITERS:
                    e0 = split_mm(jnp.concatenate(new, axis=0), w0[...])
                    put(k + 1, x, 0, e0[:NY2])
                    put(k + 1, x, 1, e0[NY2:])
            return acc

        return lax.fori_loop(0, NXL // ROWS, body, jnp.zeros((8, 128), F32))

    for j in range(ITERS):
        k = 3 * j
        receive(k)
        coarse_pass(k)
        correct_pass(k)
        send(k + 1)
        mean_step(j)
        receive(k + 1)
        acc = smooth_pass(k + 1, j)
        send(k + 2)
        nus[2 * j] = acc + nu0 if j == 0 else acc
        receive(k + 2)
        nus[2 * j + 1] = next_pass(k + 2, j)
        if j + 1 < ITERS:
            send(k + 3)

    rows = lax.broadcasted_iota(jnp.int32, (8, 128), 0)
    part = jnp.zeros((8, 128), F32)
    for n in range(2 * ITERS):
        rho, y = local(bars[(n + 1) // 2]), local(ybars[n // 2])
        v = nus[n] + 128.0 * jnp.sum((rho * y).reshape(4, 8, 128), axis=0)
        part = part + jnp.where(rows == n, jnp.sum(v, axis=0, keepdims=True), 0.0)
    red1[0] = part

    def sum_copies(buf, send_sems, recv_sems, devs):
        return [
            pltpu.make_async_remote_copy(
                src_ref=buf.at[0], dst_ref=buf.at[i + 1], send_sem=send_sems.at[i],
                recv_sem=recv_sems.at[i], device_id=dev, device_id_type=MESH,
            )
            for i, dev in enumerate(devs)
        ]

    def sum_phase(copies, buf):
        for copy in copies:
            copy.start()
        for copy in copies:
            copy.wait_recv()
        total = buf[0]
        for i in range(len(copies)):
            total = total + buf[i + 1]
        return total

    copies1 = sum_copies(red1, s1_sem, r1_sem, [first_dev(*d) for d in first])
    red2[0] = sum_phase(copies1, red1)
    copies2 = sum_copies(red2, s2_sem, r2_sem, [second_dev(d) for d in second])
    total = sum_phase(copies2, red2)
    total = jnp.broadcast_to(jnp.sum(total, axis=1, keepdims=True), (8, 128))
    nu = [total[n : n + 1] for n in range(2 * ITERS)]

    h00, h10, h20 = nu[0] - nu[1], nu[1] - nu[2], nu[2] - nu[3]
    h11, h21, h22 = nu[2] - nu[3], nu[3] - nu[4], nu[4] - nu[5]
    l10, l20 = h10 / h00, h20 / h00
    d1, s21 = h11 - l10 * h10, h21 - l10 * h20
    l21 = s21 / d1
    d2 = h22 - l20 * h20 - l21 * s21
    b1 = nu[1] - l10 * nu[0]
    b2 = nu[2] - l20 * nu[0] - l21 * b1
    c2 = b2 / d2
    c1 = b1 / d1 - l21 * c2
    c0 = nu[0] / h00 - l10 * c1 - l20 * c2
    a0, a1, a2 = 1.0 - c0, c0 - c1, c1 - c2

    xbar = c0 * local(ybars[0]) + c1 * local(ybars[1]) + c2 * local(ybars[2])
    rbar = a1 * local(bars[1]) + a2 * local(bars[2]) + c2 * local(bars[3])
    to_columns(xbar)
    xcols = [tmat[pl.ds(b, NY2, stride=2), :] for b in range(2)]
    to_columns(rbar)
    rcols = [tmat[pl.ds(b, NY2, stride=2), :] for b in range(2)]

    outs = []
    for g in range(4):
        for x in range(8 * g, 8 * g + 8):
            for b in range(2):
                v = inp[x, pl.ds(b, NY2, stride=2), :]
                m = m3[x, b]
                ox = c0 * ys[0, x, b] + c1 * ys[1, x, b] + c2 * ys[2, x, b]
                ox = ox + c0 * ((1.0 - m) * v) + xcols[b][:, x : x + 1]
                orr = a0 * v + a1 * rhos[1, x, b] + a2 * rhos[2, x, b] + c2 * rhos[3, x, b]
                orr = orr + rcols[b][:, x : x + 1]
                outx[x, pl.ds(b, NY2, stride=2), :] = ox
                outr[x, pl.ds(b, NY2, stride=2), :] = orr
        cells = pl.ds(8 * g, 8)
        for i, (src, dst) in enumerate(((outx, x_ref), (outr, r_ref))):
            copy = pltpu.make_async_copy(src.at[cells], dst.at[cells], out_sem.at[i, g])
            copy.start()
            outs.append(copy)

    for i in range(8):
        pl.when(exists(*SIDES[i]))(lambda i=i: block_copy(i).wait_send())
    for k in range(3 * ITERS):
        for copy, there, _ in faces(k):
            pl.when(there)(copy.wait_send)
    for copy in copies1 + copies2:
        copy.wait_send()
    for copy in outs:
        copy.wait()


def shards(nx, ny, right_side, sea_mask, vertical_coupling):
    vmem = pltpu.VMEM
    ng = nx // 4
    n_first = 4 * ny - 1
    out = jax.ShapeDtypeStruct(right_side.shape, F32)
    return pl.pallas_call(
        functools.partial(kernel, nx, ny),
        out_shape=(out, out),
        in_specs=[
            pl.BlockSpec(memory_space=pl.ANY),
            pl.BlockSpec(memory_space=vmem),
            pl.BlockSpec(memory_space=vmem),
        ],
        out_specs=(pl.BlockSpec(memory_space=pl.ANY), pl.BlockSpec(memory_space=pl.ANY)),
        scratch_shapes=[
            vmem((NXL, 128, 128), F32),
            vmem((NXL, 128, 128), F32),
            vmem((NXL, 128, 128), F32),
            vmem((3 * ITERS, NXL + 2, 2, 80, 128), F32),
            vmem((ITERS, NXL, 2, NY2, 128), F32),
            vmem((ITERS + 1, NXL, 2, NY2, 128), F32),
            vmem((NXL, 2, NY2, 128), F32),
            vmem((NXL, 2, NY2, 128), F32),
            vmem((NXL // 2, NY2, 128), F32),
            vmem((NXL // 2, NY2, 128), F32),
            vmem((3 * ITERS, 2, NXL, 128), F32),
            vmem((3 * ITERS, 2, NXL, 128), F32),
            vmem((256, 256), BF16),
            vmem((256, 256), BF16),
            vmem((1, 128), F32),
            vmem((2 * NXL, 128), F32),
            vmem((8, 2 * NXL, 128), F32),
            vmem((128, 128), F32),
            vmem((4, 96, 256), F32),
            vmem((96, 256), F32),
            vmem((ITERS + 1, 96, 256), F32),
            vmem((ITERS, 96, 256), F32),
            vmem((2 * ITERS, 8, 128), F32),
            vmem((n_first + 1, 8, 128), F32),
            vmem((ng, 8, 128), F32),
            pltpu.SemaphoreType.DMA,
            pltpu.SemaphoreType.DMA((2, 4)),
            pltpu.SemaphoreType.DMA((3 * ITERS, 4)),
            pltpu.SemaphoreType.DMA((3 * ITERS, 4)),
            pltpu.SemaphoreType.DMA((8,)),
            pltpu.SemaphoreType.DMA((8,)),
            pltpu.SemaphoreType.DMA((n_first,)),
            pltpu.SemaphoreType.DMA((n_first,)),
            pltpu.SemaphoreType.DMA((ng - 1,)),
            pltpu.SemaphoreType.DMA((ng - 1,)),
        ],
        compiler_params=pltpu.CompilerParams(
            collective_id=0, has_side_effects=True, vmem_limit_bytes=60 * 1024 * 1024
        ),
    )(right_side, sea_mask, vertical_coupling.reshape(1, -1))


def solution(mesh):
    nx, ny = mesh.shape["gx"], mesh.shape["gy"]
    return jax.shard_map(
        functools.partial(shards, nx, ny),
        mesh=mesh,
        in_specs=(P("gx", "gy", None), P("gx", "gy"), P()),
        out_specs=(P("gx", "gy", None), P("gx", "gy", None)),
        check_vma=False,
    )
```

```python
import functools

import jax
import jax.numpy as jnp
from jax import lax
from jax.experimental import pallas as pl
from jax.experimental.pallas import tpu as pltpu
from jax.sharding import PartitionSpec as P


ITERS = 3
SWEEPS = 4
F32 = jnp.float32
BF16 = jnp.bfloat16
MESH = pl.DeviceIdType.MESH
NXL, NY2, NZ = 32, 64, 128
ROWS = 8
HALO = 3
SIDES = [(dx, dy) for dx in (-1, 0, 1) for dy in (-1, 0, 1) if (dx, dy) != (0, 0)]


def split_mm(v, w):
    high = v.astype(BF16)
    low = (v - high.astype(F32)).astype(BF16)
    o = jnp.dot(jnp.concatenate([high, low], axis=1), w, preferred_element_type=F32)
    return o[:, :128] + o[:, 128:]


def roll(v, shift, axis):
    return pltpu.roll(v, shift % v.shape[axis], axis)


def line_inverses(coupling, w_refs):
    lane = lax.broadcasted_iota(jnp.int32, (8, 128), 1)
    row = lax.broadcasted_iota(jnp.int32, (8, 128), 0)
    up = jnp.broadcast_to(coupling, (8, 128))
    lo = roll(up, 1, 1)
    factor = jnp.where(row == 0, 1.0, 4.0)
    diag = jnp.where(row == 0, 4.1, 4.4) + factor * (up + lo)
    off_up = factor * up
    off_lo = factor * lo

    def pivots(off, step):
        a, b = diag, -off * off
        c, d = jnp.ones_like(a), jnp.zeros_like(a)
        s = 1
        while s < 128:
            inside = (lane >= s) if step > 0 else (lane < 128 - s)
            ra = jnp.where(inside, roll(a, step * s, 1), 1.0)
            rb = jnp.where(inside, roll(b, step * s, 1), 0.0)
            rc = jnp.where(inside, roll(c, step * s, 1), 0.0)
            rd = jnp.where(inside, roll(d, step * s, 1), 1.0)
            na, nb = a * ra + b * rc, a * rb + b * rd
            nc, nd = c * ra + d * rc, c * rb + d * rd
            inv = 1.0 / na
            a, b, c, d = jnp.ones_like(a), nb * inv, nc * inv, nd * inv
            s *= 2
        return 1.0 / c

    fore = pivots(off_lo, 1)
    back = pivots(off_up, -1)
    main = 1.0 / (fore + back - diag)
    ratio = jnp.where(lane < 127, jnp.log(jnp.maximum(off_up, 1e-30) / fore), 0.0)
    total = jnp.where(lane >= 1, roll(ratio, 1, 1), 0.0)
    s = 1
    while s < 128:
        total = total + jnp.where(lane >= s, roll(total, s, 1), 0.0)
        s *= 2

    r = lax.broadcasted_iota(jnp.int32, (128, 128), 0)
    c = lax.broadcasted_iota(jnp.int32, (128, 128), 1)
    for i, w_ref in enumerate(w_refs):
        def wide(v):
            return jnp.broadcast_to(v[i : i + 1], (128, 128))

        g_row, t_row = wide(main), wide(total)
        g_col, t_col = g_row.T, t_row.T
        g = jnp.where(r <= c, g_row, g_col) * jnp.exp(-jnp.abs(t_row - t_col))
        a_col, u_col = wide(diag).T, wide(off_up).T
        l_col = wide(off_lo).T
        tg = a_col * g - u_col * roll(g, -1, 0) - l_col * roll(g, 1, 0)
        rest = jnp.where(r == c, 1.0, 0.0) - tg
        g = g + jnp.dot(g.astype(BF16), rest.astype(BF16), preferred_element_type=F32)
        high = g.astype(BF16)
        low = (g - high.astype(F32)).astype(BF16)
        both = jnp.concatenate([high, low], axis=1)
        w_ref[...] = jnp.concatenate([both, both], axis=0)


def kernel(
    nx, ny, rhs_ref, mask_ref, coup_ref, x_ref, r_ref,
    inp, outx, outr, rho0, rho1, rho2, rho3, y0, y1, y2, e0b, eb, db, h1s, m3, q3,
    sr, ss, se0, se, sd, cb0, cb, sm, sq, w0, w1, kpad,
    blk, nbr, tmat, mn, m2, bars, ybars, nus, red1, red2,
    in_sem, out_sem, sx_sem, rx_sem, sb_sem, rb_sem, s1_sem, r1_sem, s2_sem, r2_sem,
):
    gx, gy = lax.axis_index("gx"), lax.axis_index("gy")
    lo, hi = lax.rem(gx, 4), lax.div(gx, 4)
    ng = nx // 4
    rhos, ys = (rho0, rho1, rho2, rho3), (y0, y1, y2)

    first = [(dl, dg) for dl in range(4) for dg in range(ny) if (dl, dg) != (0, 0)]
    second = list(range(1, ng))

    def first_dev(dl, dg):
        return (hi * 4 + lax.rem(lo + dl, 4), lax.rem(gy + dg, ny))

    def second_dev(dh):
        return (lax.rem(hi + dh, ng) * 4 + lo, gy)

    def side_dev(dx, dy):
        return (lax.rem(gx + dx + nx, nx), lax.rem(gy + dy + ny, ny))

    load = pltpu.make_async_copy(rhs_ref, inp, in_sem)
    load.start()

    def clear(x, carry):
        zero = jnp.zeros((2, NY2, 128), F32)
        for rho in (rho0, rho1, rho2):
            rho[x] = zero
            rho[x + NXL + HALO] = zero
        return carry

    lax.fori_loop(0, HALO, clear, 0)
    sr[...] = jnp.zeros(sr.shape, F32)
    nbr[...] = jnp.zeros(nbr.shape, F32)
    cb0[...] = jnp.zeros(cb0.shape, F32)
    cb[...] = jnp.zeros(cb.shape, F32)

    barrier = pltpu.get_barrier_semaphore()
    for dx, dy in SIDES:
        pl.semaphore_signal(barrier, inc=1, device_id=side_dev(dx, dy), device_id_type=MESH)
    for dl, dg in first:
        pl.semaphore_signal(barrier, inc=1, device_id=first_dev(dl, dg), device_id_type=MESH)
    for dh in second:
        pl.semaphore_signal(barrier, inc=1, device_id=second_dev(dh), device_id_type=MESH)

    kpad[...] = jnp.zeros((1, 128), F32)
    kpad[:, 0:127] = coup_ref[...]
    line_inverses(kpad[...], (w0, w1))

    lane = lax.broadcasted_iota(jnp.int32, (NY2, 128), 1)

    def to_columns(v):
        tmat[...] = jnp.concatenate([v, jnp.zeros((128 - v.shape[0], 128), F32)], axis=0).T

    def expand(dst, start, stop, shift):
        for b in range(2):
            col = tmat[pl.ds(b, NY2, stride=2), :]
            for x in range(start, stop):
                dst[x + shift, b] = jnp.broadcast_to(col[:, x : x + 1], (NY2, 128))

    mask = mask_ref[...].astype(F32)
    blk[0:NXL, :] = mask
    to_columns(mask)
    expand(m3, 0, NXL, 2)

    def put_sides(dst, x, b, v):
        if b == 0:
            dst[0, 0, pl.ds(x, 1), :] = v[0:1]
            dst[0, 2, pl.ds(x, 1), :] = v[1:2]
            dst[1, 1, pl.ds(x, 1), :] = v[NY2 - 1 : NY2]
        else:
            dst[0, 1, pl.ds(x, 1), :] = v[0:1]
            dst[1, 0, pl.ds(x, 1), :] = v[NY2 - 1 : NY2]
            dst[1, 2, pl.ds(x, 1), :] = v[NY2 - 2 : NY2 - 1]

    def put(dst, edge, shift, x, b, v):
        dst[x + shift, b, 8:72, :] = v
        if edge is not None:
            row = v[0:1] if b == 0 else v[NY2 - 1 : NY2]
            edge[b, pl.ds(x + 8, 1), :] = row

    def tile_sum(v):
        return jnp.sum(v.reshape(8, 8, 128), axis=0)

    load.wait()

    def start_pass(x, carry):
        acc, means = carry[0], list(carry[1:])
        for b in range(2):
            v = inp[x, pl.ds(b, NY2, stride=2), :]
            m = m3[x + 2, b]
            mean = jnp.sum(v, axis=1, keepdims=True) * (1.0 / NZ)
            means[b] = jnp.where(lane == x, mean, means[b])
            dev = m * (v - mean)
            rho0[x + HALO, b] = dev
            put_sides(ss.at[0], x, b, dev)
            land = (1.0 - m) * v
            acc = acc + tile_sum(land * land)
        return (acc, *means)

    zero = jnp.zeros((NY2, 128), F32)
    nu0, mean0, mean1 = lax.fori_loop(0, NXL, start_pass, (jnp.zeros((8, 128), F32), zero, zero))
    tmat[pl.ds(0, NY2, stride=2), :] = mean0
    tmat[pl.ds(1, NY2, stride=2), :] = mean1
    blk[NXL : 2 * NXL, :] = mask * tmat[...].T[0:NXL]

    pl.semaphore_wait(barrier, len(SIDES) + len(first) + len(second))

    def exists(dx, dy):
        ok = None
        for pos, d, n in ((gx, dx, nx), (gy, dy, ny)):
            if d:
                here = (pos + d >= 0) & (pos + d < n)
                ok = here if ok is None else ok & here
        return ok

    def block_copy(i):
        return pltpu.make_async_remote_copy(
            src_ref=blk, dst_ref=nbr.at[i], send_sem=sb_sem.at[i], recv_sem=rb_sem.at[i],
            device_id=side_dev(*SIDES[i]), device_id_type=MESH,
        )

    def face(j, i):
        dx, dy = SIDES[i]
        if dy == 0:
            src = rhos[j].at[pl.ds(HALO if dx < 0 else NXL, HALO)]
            dst = rhos[j].at[pl.ds(NXL + HALO if dx < 0 else 0, HALO)]
        else:
            s = 0 if dy < 0 else 1
            x0, n, to = {-1: (0, 8, 40), 0: (0, NXL, 8), 1: (NXL - 8, 8, 0)}[dx]
            src = ss.at[j, s, :, pl.ds(x0, n), :]
            dst = sr.at[j, 1 - s, :, pl.ds(to, n), :]
        return pltpu.make_async_remote_copy(
            src_ref=src, dst_ref=dst, send_sem=sx_sem.at[j, i], recv_sem=rx_sem.at[j, i],
            device_id=side_dev(dx, dy), device_id_type=MESH,
        )

    along_x = [i for i, (dx, dy) in enumerate(SIDES) if dy == 0]
    along_y = [i for i, (dx, dy) in enumerate(SIDES) if dx == 0]
    corners = [i for i, (dx, dy) in enumerate(SIDES) if dx and dy]

    def send(j, which):
        for i in which:
            pl.when(exists(*SIDES[i]))(lambda i=i: face(j, i).start())

    def receive(j):
        for i, (dx, dy) in enumerate(SIDES):
            pl.when(exists(-dx, -dy))(lambda i=i: face(j, i).wait_recv())

    for i in corners + along_x + along_y:
        pl.when(exists(*SIDES[i]))(lambda i=i: block_copy(i).start())
    send(0, along_x + corners + along_y)

    def line_pass0(i, carry):
        for x8 in range(ROWS):
            x = i * ROWS + x8
            e0 = split_mm(rho0[x + HALO].reshape(128, 128), w0[...])
            put(e0b, cb0, HALO, x, 0, e0[:NY2])
            put(e0b, cb0, HALO, x, 1, e0[NY2:])
        return carry

    lax.fori_loop(0, NXL // ROWS, line_pass0, 0)

    for i in range(8):
        dx, dy = SIDES[i]
        pl.when(exists(-dx, -dy))(lambda i=i: block_copy(i).wait_recv())

    low_half = lax.broadcasted_iota(jnp.int32, (96, 128), 1) < 64

    def around(rows):
        def column(dy):
            parts = []
            for dx in (-1, 0, 1):
                if (dx, dy) == (0, 0):
                    parts.append(blk[rows, :])
                else:
                    parts.append(nbr[SIDES.index((-dx, -dy)), rows, :])
            return roll(jnp.concatenate(parts, axis=0), 64, 1)

        left, mid, right = column(-1), column(0), column(1)
        return jnp.concatenate(
            [jnp.where(low_half, left, mid), jnp.where(low_half, mid, right)], axis=1
        )

    def local(v):
        a, b = roll(v[:, 0:128], 64, 1), roll(v[:, 128:256], 64, 1)
        return jnp.where(low_half[: v.shape[0]], a, b)

    moves = ((-1, 0), (1, 0), (-1, 1), (1, 1))
    mask2 = around(pl.ds(0, NXL))
    m2[...] = mask2
    bars[0] = around(pl.ds(NXL, NXL))
    open_sides = jnp.zeros((96, 256), F32)
    for i, (s, axis) in enumerate(moves):
        beside = roll(mask2, s, axis)
        mn[i] = beside
        open_sides = open_sides + beside
    own2 = mask2 * (4.0 - open_sides)
    to_columns(local(mask2[24:72]))
    expand(m3, 6, 8, -6)
    expand(m3, 40, 42, -6)
    to_columns(local(own2[24:72]))
    expand(q3, 6, 42, -6)
    for a in range(2):
        for s, at in ((0, 63 - a), (1, 192 + a)):
            sm[s, a] = jnp.broadcast_to(mask2[24:72, at : at + 1], (48, 128))
            sq[s, a] = jnp.broadcast_to(own2[24:72, at : at + 1], (48, 128))

    xi = lax.broadcasted_iota(jnp.int32, (96, 256), 0) + (gx * NXL - 32)
    yi = lax.broadcasted_iota(jnp.int32, (96, 256), 1) + (gy * 128 - 64)
    inside = (xi >= 0) & (xi < nx * NXL) & (yi >= 0) & (yi < ny * 128)
    dom = jnp.where(inside, 1.0, 0.0)

    even_x = lax.rem(lax.broadcasted_iota(jnp.int32, (96, 256), 0), 2) == 0
    even_y = lax.rem(lax.broadcasted_iota(jnp.int32, (96, 256), 1), 2) == 0
    even_s = lax.rem(lax.broadcasted_iota(jnp.int32, (48, 128), 0), 2) == 0

    def flow(v):
        total = None
        for i, (s, axis) in enumerate(moves):
            term = mn[i] * (roll(v, s, axis) - v)
            total = term if total is None else total + term
        return total

    def mean_step(j):
        m = m2[...]
        e0 = bars[j] * (1.0 / 4.1)
        t = 4.0 * e0 + flow(e0)
        t1 = m * t
        t1 = t1 + jnp.where(even_x, roll(t1, -1, 0), roll(t1, 1, 0))
        t1 = t1 + jnp.where(even_y, roll(t1, -1, 1), roll(t1, 1, 1))
        e1 = t1 * (1.0 / 4.4)
        c = (0.8 / 4.4) * t1
        for _ in range(SWEEPS - 1):
            beside = (roll(c, 2, 0) + roll(c, -2, 0)) + (roll(c, 2, 1) + roll(c, -2, 1))
            c = dom * (c + 0.8 * (t1 - (4.4 * c - beside)) / 4.4)
        f = e1 + c
        rem = m * (t + flow(f) + (e1 - 0.25 * t1) - 0.1 * c)
        d = rem * (1.0 / 4.1)
        ybars[j] = e0 + m * f + d
        bars[j + 1] = m * (4.0 * d + flow(d))

    def insert(dst, src, shift, x):
        dst[x + shift, 1, 7:8, :] = src[0, pl.ds(x + 8, 1), :]
        dst[x + shift, 0, 72:73, :] = src[1, pl.ds(x + 8, 1), :]

    def stencil(src, shift, x, b, less=None):
        mate = src[x + shift, 1 - b, 8:72, :]
        side = src[x + shift, 1 - b, 7:71, :] if b == 0 else src[x + shift, 1 - b, 9:73, :]
        beside = (src[x + shift - 1, b, 8:72, :] + src[x + shift + 1, b, 8:72, :]) + (mate + side)
        if less is not None:
            beside = beside - less
        return q3[x + 2, b] * src[x + shift, b, 8:72, :] + m3[x + 2, b] * beside

    def strip_beside(v):
        return roll(v, 1, 0) + roll(v, -1, 0)

    def halo_lines(j):
        for x in (-3, -2, -1, 32, 33, 34):
            e0 = split_mm(rhos[j][x + HALO].reshape(128, 128), w0[...])
            put(e0b, cb0, HALO, x, 0, e0[:NY2])
            put(e0b, cb0, HALO, x, 1, e0[NY2:])
        se0[...] = split_mm(sr[j].reshape(288, 128), w0[...]).reshape(2, 3, 48, 128)

    def strip_correct():
        t1 = []
        for s in range(2):
            near, mid, far = se0[s, 0], se0[s, 1], se0[s, 2]
            t = sq[s, 0] * near + sm[s, 0] * (cb0[s] + mid + strip_beside(near))
            t = t + sq[s, 1] * mid + sm[s, 1] * (near + far + strip_beside(mid))
            t1.append(t + jnp.where(even_s, roll(t, -1, 0), roll(t, 1, 0)))
        t1 = jnp.concatenate(t1, axis=0)
        e1 = split_mm(t1, w1[...])
        h1 = 0.25 * t1 + 3.0 * e1
        for s in range(2):
            part = e1[48 * s : 48 * s + 48]
            for a in range(2):
                se[s, a] = se0[s, a] + sm[s, a] * part
            sd[s] = h1[48 * s : 48 * s + 48]

    def strip_smooth():
        rem = []
        for s in range(2):
            near, far = se[s, 0], se[s, 1]
            rem.append(sq[s, 0] * near + sm[s, 0] * (cb[s] + far + strip_beside(near) - sd[s]))
        sd[...] = split_mm(jnp.concatenate(rem, axis=0), w0[...]).reshape(2, 48, 128)

    def correct_pass():
        def body(i, carry):
            t1 = []
            for k in range(6):
                x2 = i * 6 + k
                total = None
                for x in (2 * x2 - 2, 2 * x2 - 1):
                    insert(e0b, se0.at[:, 0], HALO, x)
                    for b in range(2):
                        t = stencil(e0b, HALO, x, b)
                        total = t if total is None else total + t
                t1.append(total)
            t1 = jnp.concatenate(t1, axis=0)
            e1 = split_mm(t1, w1[...])
            h1s[pl.ds(i * 6, 6)] = (0.25 * t1 + 3.0 * e1).reshape(6, NY2, 128)
            for k in range(6):
                x2 = i * 6 + k
                part = e1[k * NY2 : (k + 1) * NY2]
                for x in (2 * x2 - 2, 2 * x2 - 1):
                    for b in range(2):
                        v = e0b[x + HALO, b, 8:72, :] + m3[x + 2, b] * part
                        put(eb, cb, HALO, x, b, v)
            return carry

        lax.fori_loop(0, 3, body, 0)

    def smooth_row(x, half):
        insert(eb, se.at[:, 0], HALO, x)
        rem = [stencil(eb, HALO, x, b, h1s[half + 1]) for b in range(2)]
        return split_mm(jnp.concatenate(rem, axis=0), w0[...])

    def smooth_pass(j):
        for x, half in ((-1, -1), (NXL, NXL // 2)):
            d = smooth_row(x, half)
            for b in range(2):
                put(db, None, 1, x, b, d[b * NY2 : (b + 1) * NY2])

        def body(i, acc):
            for x8 in range(ROWS):
                x = i * ROWS + x8
                d = smooth_row(x, i * (ROWS // 2) + x8 // 2)
                for b in range(2):
                    part = d[b * NY2 : (b + 1) * NY2]
                    y = eb[x + HALO, b, 8:72, :] + part
                    put(db, None, 1, x, b, part)
                    ys[j][x, b] = y
                    acc = acc + tile_sum(rhos[j][x + HALO, b] * y)
            return acc

        return lax.fori_loop(0, NXL // ROWS, body, jnp.zeros((8, 128), F32))

    def next_pass(j):
        shift = HALO if j + 1 < ITERS else 0

        def rows(i, acc):
            for x8 in range(ROWS):
                x = i * ROWS + x8
                insert(db, sd, 1, x)
                new = []
                for b in range(2):
                    v = stencil(db, 1, x, b)
                    rhos[j + 1][x + shift, b] = v
                    acc = acc + tile_sum(v * ys[j][x, b])
                    new.append(v)
                    if j + 1 < ITERS:
                        put_sides(ss.at[j + 1], x, b, v)
                if j + 1 < ITERS:
                    e0 = split_mm(jnp.concatenate(new, axis=0), w0[...])
                    put(e0b, cb0, HALO, x, 0, e0[:NY2])
                    put(e0b, cb0, HALO, x, 1, e0[NY2:])
            return acc

        last = NXL // ROWS - 1
        acc = lax.fori_loop(0, 2, lambda i, a: rows(i * last, a), jnp.zeros((8, 128), F32))
        if j + 1 < ITERS:
            send(j + 1, along_x + corners)
        acc = lax.fori_loop(1, last, rows, acc)
        if j + 1 < ITERS:
            send(j + 1, along_y)
        return acc

    for j in range(ITERS):
        receive(j)
        halo_lines(j)
        strip_correct()
        correct_pass()
        strip_smooth()
        acc = smooth_pass(j)
        nus[2 * j] = acc + nu0 if j == 0 else acc
        nus[2 * j + 1] = next_pass(j)
        if j == 0:
            mean_step(0)
            mean_step(1)
        if j == 1:
            mean_step(2)

    rows = lax.broadcasted_iota(jnp.int32, (8, 128), 0)
    part = jnp.zeros((8, 128), F32)
    here = pl.ds(32, NXL)
    for n in range(2 * ITERS):
        rho, y = local(bars[(n + 1) // 2, here]), local(ybars[n // 2, here])
        v = nus[n] + 128.0 * jnp.sum((rho * y).reshape(4, 8, 128), axis=0)
        part = part + jnp.where(rows == n, jnp.sum(v, axis=0, keepdims=True), 0.0)
    red1[0] = part

    def sum_copies(buf, send_sems, recv_sems, devs):
        return [
            pltpu.make_async_remote_copy(
                src_ref=buf.at[0], dst_ref=buf.at[i + 1], send_sem=send_sems.at[i],
                recv_sem=recv_sems.at[i], device_id=dev, device_id_type=MESH,
            )
            for i, dev in enumerate(devs)
        ]

    def sum_phase(copies, buf):
        for copy in copies:
            copy.start()
        for copy in copies:
            copy.wait_recv()
        total = buf[0]
        for i in range(len(copies)):
            total = total + buf[i + 1]
        return total

    copies1 = sum_copies(red1, s1_sem, r1_sem, [first_dev(*d) for d in first])
    red2[0] = sum_phase(copies1, red1)
    copies2 = sum_copies(red2, s2_sem, r2_sem, [second_dev(d) for d in second])
    total = sum_phase(copies2, red2)
    total = jnp.broadcast_to(jnp.sum(total, axis=1, keepdims=True), (8, 128))
    nu = [total[n : n + 1] for n in range(2 * ITERS)]

    h00, h10, h20 = nu[0] - nu[1], nu[1] - nu[2], nu[2] - nu[3]
    h11, h21, h22 = nu[2] - nu[3], nu[3] - nu[4], nu[4] - nu[5]
    l10, l20 = h10 / h00, h20 / h00
    d1, s21 = h11 - l10 * h10, h21 - l10 * h20
    l21 = s21 / d1
    d2 = h22 - l20 * h20 - l21 * s21
    b1 = nu[1] - l10 * nu[0]
    b2 = nu[2] - l20 * nu[0] - l21 * b1
    c2 = b2 / d2
    c1 = b1 / d1 - l21 * c2
    c0 = nu[0] / h00 - l10 * c1 - l20 * c2
    a0, a1, a2 = 1.0 - c0, c0 - c1, c1 - c2

    xbar = c0 * local(ybars[0, here]) + c1 * local(ybars[1, here]) + c2 * local(ybars[2, here])
    rbar = a1 * local(bars[1, here]) + a2 * local(bars[2, here]) + c2 * local(bars[3, here])
    to_columns(xbar)
    xcols = [tmat[pl.ds(b, NY2, stride=2), :] for b in range(2)]
    to_columns(rbar)
    rcols = [tmat[pl.ds(b, NY2, stride=2), :] for b in range(2)]

    outs = []
    for g in range(4):
        for x in range(8 * g, 8 * g + 8):
            for b in range(2):
                v = inp[x, pl.ds(b, NY2, stride=2), :]
                m = m3[x + 2, b]
                ox = c0 * y0[x, b] + c1 * y1[x, b] + c2 * y2[x, b]
                ox = ox + c0 * ((1.0 - m) * v) + xcols[b][:, x : x + 1]
                orr = a0 * v + a1 * rho1[x + HALO, b] + a2 * rho2[x + HALO, b] + c2 * rho3[x, b]
                orr = orr + rcols[b][:, x : x + 1]
                outx[x, pl.ds(b, NY2, stride=2), :] = ox
                outr[x, pl.ds(b, NY2, stride=2), :] = orr
        cells = pl.ds(8 * g, 8)
        for i, (src, dst) in enumerate(((outx, x_ref), (outr, r_ref))):
            copy = pltpu.make_async_copy(src.at[cells], dst.at[cells], out_sem.at[i, g])
            copy.start()
            outs.append(copy)

    for i in range(8):
        pl.when(exists(*SIDES[i]))(lambda i=i: block_copy(i).wait_send())
        for j in range(ITERS):
            pl.when(exists(*SIDES[i]))(lambda i=i, j=j: face(j, i).wait_send())
    for copy in copies1 + copies2:
        copy.wait_send()
    for copy in outs:
        copy.wait()


def shards(nx, ny, right_side, sea_mask, vertical_coupling):
    vmem = pltpu.VMEM
    ng = nx // 4
    n_first = 4 * ny - 1
    out = jax.ShapeDtypeStruct(right_side.shape, F32)
    return pl.pallas_call(
        functools.partial(kernel, nx, ny),
        out_shape=(out, out),
        in_specs=[
            pl.BlockSpec(memory_space=pl.ANY),
            pl.BlockSpec(memory_space=vmem),
            pl.BlockSpec(memory_space=vmem),
        ],
        out_specs=(pl.BlockSpec(memory_space=pl.ANY), pl.BlockSpec(memory_space=pl.ANY)),
        scratch_shapes=[
            vmem((NXL, 128, 128), F32),
            vmem((NXL, 128, 128), F32),
            vmem((NXL, 128, 128), F32),
            vmem((NXL + 2 * HALO, 2, NY2, 128), F32),
            vmem((NXL + 2 * HALO, 2, NY2, 128), F32),
            vmem((NXL + 2 * HALO, 2, NY2, 128), F32),
            vmem((NXL, 2, NY2, 128), F32),
            vmem((NXL, 2, NY2, 128), F32),
            vmem((NXL, 2, NY2, 128), F32),
            vmem((NXL, 2, NY2, 128), F32),
            vmem((NXL + 2 * HALO, 2, 80, 128), F32),
            vmem((NXL + 2 * HALO, 2, 80, 128), F32),
            vmem((NXL + 2, 2, 80, 128), F32),
            vmem((NXL // 2 + 2, NY2, 128), F32),
            vmem((NXL + 4, 2, NY2, 128), F32),
            vmem((NXL + 4, 2, NY2, 128), F32),
            vmem((ITERS, 2, 3, 48, 128), F32),
            vmem((ITERS, 2, 3, NXL, 128), F32),
            vmem((2, 3, 48, 128), F32),
            vmem((2, 2, 48, 128), F32),
            vmem((2, 48, 128), F32),
            vmem((2, 48, 128), F32),
            vmem((2, 48, 128), F32),
            vmem((2, 2, 48, 128), F32),
            vmem((2, 2, 48, 128), F32),
            vmem((256, 256), BF16),
            vmem((256, 256), BF16),
            vmem((1, 128), F32),
            vmem((2 * NXL, 128), F32),
            vmem((8, 2 * NXL, 128), F32),
            vmem((128, 128), F32),
            vmem((4, 96, 256), F32),
            vmem((96, 256), F32),
            vmem((ITERS + 1, 96, 256), F32),
            vmem((ITERS, 96, 256), F32),
            vmem((2 * ITERS, 8, 128), F32),
            vmem((n_first + 1, 8, 128), F32),
            vmem((ng, 8, 128), F32),
            pltpu.SemaphoreType.DMA,
            pltpu.SemaphoreType.DMA((2, 4)),
            pltpu.SemaphoreType.DMA((ITERS, 8)),
            pltpu.SemaphoreType.DMA((ITERS, 8)),
            pltpu.SemaphoreType.DMA((8,)),
            pltpu.SemaphoreType.DMA((8,)),
            pltpu.SemaphoreType.DMA((n_first,)),
            pltpu.SemaphoreType.DMA((n_first,)),
            pltpu.SemaphoreType.DMA((ng - 1,)),
            pltpu.SemaphoreType.DMA((ng - 1,)),
        ],
        compiler_params=pltpu.CompilerParams(
            collective_id=0, has_side_effects=True, vmem_limit_bytes=60 * 1024 * 1024
        ),
    )(right_side, sea_mask, vertical_coupling.reshape(1, -1))


def solution(mesh):
    nx, ny = mesh.shape["gx"], mesh.shape["gy"]
    return jax.shard_map(
        functools.partial(shards, nx, ny),
        mesh=mesh,
        in_specs=(P("gx", "gy", None), P("gx", "gy"), P()),
        out_specs=(P("gx", "gy", None), P("gx", "gy", None)),
        check_vma=False,
    )
```

```python
import functools
import itertools
import math

import jax
import jax.numpy as jnp
from jax import lax
from jax.experimental import pallas as pl
from jax.experimental.pallas import tpu as pltpu
from jax.sharding import PartitionSpec as P


ITERS = 3
SWEEPS = 4
F32 = jnp.float32
BF16 = jnp.bfloat16
MESH = pl.DeviceIdType.MESH
NXL, NY2, NZ = 32, 64, 128
ROWS = 8
HALO = 3
H = 32
PHASES = ("cz", "xy")
SIDES = [(dx, dy) for dx in (-1, 0, 1) for dy in (-1, 0, 1) if (dx, dy) != (0, 0)]


def split_mm(v, w):
    high = v.astype(BF16)
    low = (v - high.astype(F32)).astype(BF16)
    o = jnp.dot(jnp.concatenate([high, low], axis=1), w, preferred_element_type=F32)
    return o[:, :128] + o[:, 128:]


def roll(v, shift, axis):
    return pltpu.roll(v, shift % v.shape[axis], axis)


def line_inverses(coupling, w_refs):
    lane = lax.broadcasted_iota(jnp.int32, (8, 128), 1)
    row = lax.broadcasted_iota(jnp.int32, (8, 128), 0)
    up = jnp.broadcast_to(coupling, (8, 128))
    lo = roll(up, 1, 1)
    factor = jnp.where(row == 0, 1.0, 4.0)
    diag = jnp.where(row == 0, 4.1, 4.4) + factor * (up + lo)
    off_up = factor * up
    off_lo = factor * lo

    def pivots(off, step):
        a, b = diag, -off * off
        c, d = jnp.ones_like(a), jnp.zeros_like(a)
        s = 1
        while s < 128:
            inside = (lane >= s) if step > 0 else (lane < 128 - s)
            ra = jnp.where(inside, roll(a, step * s, 1), 1.0)
            rb = jnp.where(inside, roll(b, step * s, 1), 0.0)
            rc = jnp.where(inside, roll(c, step * s, 1), 0.0)
            rd = jnp.where(inside, roll(d, step * s, 1), 1.0)
            na, nb = a * ra + b * rc, a * rb + b * rd
            nc, nd = c * ra + d * rc, c * rb + d * rd
            inv = 1.0 / na
            a, b, c, d = jnp.ones_like(a), nb * inv, nc * inv, nd * inv
            s *= 2
        return 1.0 / c

    fore = pivots(off_lo, 1)
    back = pivots(off_up, -1)
    main = 1.0 / (fore + back - diag)
    ratio = jnp.where(lane < 127, jnp.log(jnp.maximum(off_up, 1e-30) / fore), 0.0)
    total = jnp.where(lane >= 1, roll(ratio, 1, 1), 0.0)
    s = 1
    while s < 128:
        total = total + jnp.where(lane >= s, roll(total, s, 1), 0.0)
        s *= 2

    r = lax.broadcasted_iota(jnp.int32, (128, 128), 0)
    c = lax.broadcasted_iota(jnp.int32, (128, 128), 1)
    for i, w_ref in enumerate(w_refs):
        def wide(v):
            return jnp.broadcast_to(v[i : i + 1], (128, 128))

        g_row, t_row = wide(main), wide(total)
        g_col, t_col = g_row.T, t_row.T
        g = jnp.where(r <= c, g_row, g_col) * jnp.exp(-jnp.abs(t_row - t_col))
        a_col, u_col = wide(diag).T, wide(off_up).T
        l_col = wide(off_lo).T
        tg = a_col * g - u_col * roll(g, -1, 0) - l_col * roll(g, 1, 0)
        rest = jnp.where(r == c, 1.0, 0.0) - tg
        g = g + jnp.dot(g.astype(BF16), rest.astype(BF16), preferred_element_type=F32)
        high = g.astype(BF16)
        low = (g - high.astype(F32)).astype(BF16)
        both = jnp.concatenate([high, low], axis=1)
        w_ref[...] = jnp.concatenate([both, both], axis=0)


def kernel(
    nx, ny, rhs_ref, mask_hbm, coup_hbm, x_ref, r_ref,
    mask_ref, coup_ref, inp, rho0, rho1, rho2, rho3, y0, y1, y2, e0b, eb, db, h1s, m3, q3,
    sr, ss, se0, se, sd, cb0, cb, sm, sq, w0, w1, kpad,
    blk, nbr, tmat, mn, m2, bars, ybars, nus, red0, red1, red2,
    in_sem, sx_sem, rx_sem, sb_sem, rb_sem, ss_sem, rs_sem,
):
    gx, gy = lax.axis_index("gx"), lax.axis_index("gy")
    reds = (red0, red1, red2)
    rhos, ys = (rho0, rho1, rho2, rho3), (y0, y1, y2)

    sizes = {"x": nx // 8, "y": 4, "c": 2, "z": ny}
    place = {"x": lax.div(gx, 8), "y": lax.rem(lax.div(gx, 2), 4), "c": lax.rem(gx, 2), "z": gy}

    def partners(axes):
        devs = []
        for steps in itertools.product(*(range(sizes[axis]) for axis in axes)):
            if any(steps):
                at = dict(place)
                for axis, step in zip(axes, steps):
                    at[axis] = lax.rem(place[axis] + step, sizes[axis])
                devs.append((at["x"] * 8 + at["y"] * 2 + at["c"], at["z"]))
        return devs

    phases = [partners(axes) for axes in PHASES]

    def side_dev(dx, dy):
        return (lax.rem(gx + dx + nx, nx), lax.rem(gy + dy + ny, ny))

    small = [
        pltpu.make_async_copy(coup_hbm, coup_ref, in_sem.at[0]),
        pltpu.make_async_copy(mask_hbm, mask_ref, in_sem.at[1]),
    ]
    load = pltpu.make_async_copy(rhs_ref, inp, in_sem.at[2])
    for copy in small:
        copy.start()
    load.start()

    def clear(x, carry):
        zero = jnp.zeros((2, NY2, 128), F32)
        for rho in (rho0, rho1, rho2):
            rho[x] = zero
            rho[x + NXL + HALO] = zero
        return carry

    lax.fori_loop(0, HALO, clear, 0)
    sr[...] = jnp.zeros(sr.shape, F32)
    nbr[...] = jnp.zeros(nbr.shape, F32)
    cb0[...] = jnp.zeros(cb0.shape, F32)
    cb[...] = jnp.zeros(cb.shape, F32)

    barrier = pltpu.get_barrier_semaphore()
    for dx, dy in SIDES:
        pl.semaphore_signal(barrier, inc=1, device_id=side_dev(dx, dy), device_id_type=MESH)
    for dev in sum(phases, []):
        pl.semaphore_signal(barrier, inc=1, device_id=dev, device_id_type=MESH)

    for copy in small:
        copy.wait()
    kpad[...] = jnp.zeros((1, 128), F32)
    kpad[:, 0:127] = coup_ref[...]

    lane = lax.broadcasted_iota(jnp.int32, (NY2, 128), 1)

    def to_columns(v):
        tmat[...] = jnp.concatenate([v, jnp.zeros((128 - v.shape[0], 128), F32)], axis=0).T

    def expand(dst, start, stop, shift):
        for b in range(2):
            col = tmat[pl.ds(b, NY2, stride=2), :]
            for x in range(start, stop):
                dst[x + shift, b] = jnp.broadcast_to(col[:, x : x + 1], (NY2, 128))

    mask = mask_ref[...].astype(F32)
    blk[0:NXL, :] = mask
    to_columns(mask)
    expand(m3, 0, NXL, 2)

    def put_sides(dst, x, b, v, h=None):
        n = v.shape[0]
        for half, d, row in (
            ((0, 0, 0), (0, 2, 1), (1, 1, n - 1)) if b == 0 else ((0, 1, 0), (1, 0, n - 1), (1, 2, n - 2))
        ):
            if h in (None, half):
                dst[half, d, pl.ds(x, 1), :] = v[row : row + 1]

    def put(dst, edge, shift, x, b, v, h=None):
        y0, n = (8, NY2) if h is None else (8 + H * h, H)
        dst[x + shift, b, y0 : y0 + n, :] = v
        if edge is not None and h in (None, b):
            row = v[0:1] if b == 0 else v[n - 1 : n]
            edge[b, pl.ds(x + 8, 1), :] = row

    def tile_sum(v):
        return jnp.sum(v.reshape(-1, 8, 128), axis=0)

    load.wait()

    def start_pass(i, carry):
        acc, means = carry[0], list(carry[1:])
        for x, b in [(i * 4 + k, b) for k in range(4) for b in range(2)]:
            v = inp[x, pl.ds(b, NY2, stride=2), :]
            m = m3[x + 2, b]
            mean = jnp.sum(v, axis=1, keepdims=True) * (1.0 / NZ)
            means[b] = jnp.where(lane == x, mean, means[b])
            dev = m * (v - mean)
            rho0[x + HALO, b] = dev
            put_sides(ss.at[0], x, b, dev)
            land = (1.0 - m) * v
            acc = acc + tile_sum(land * land)
        return (acc, *means)

    zero = jnp.zeros((NY2, 128), F32)
    nu0, mean0, mean1 = lax.fori_loop(0, NXL // 4, start_pass, (jnp.zeros((8, 128), F32), zero, zero))
    tmat[pl.ds(0, NY2, stride=2), :] = mean0
    tmat[pl.ds(1, NY2, stride=2), :] = mean1
    blk[NXL : 2 * NXL, :] = mask * tmat[...].T[0:NXL]

    pl.semaphore_wait(barrier, len(SIDES) + sum(map(len, phases)))

    def exists(dx, dy):
        ok = None
        for pos, d, n in ((gx, dx, nx), (gy, dy, ny)):
            if d:
                here = (pos + d >= 0) & (pos + d < n)
                ok = here if ok is None else ok & here
        return ok

    def block_copy(i):
        return pltpu.make_async_remote_copy(
            src_ref=blk, dst_ref=nbr.at[i], send_sem=sb_sem.at[i], recv_sem=rb_sem.at[i],
            device_id=side_dev(*SIDES[i]), device_id_type=MESH,
        )

    def face(j, i):
        dx, dy = SIDES[i]
        if dy == 0:
            src = rhos[j].at[pl.ds(HALO if dx < 0 else NXL, HALO)]
            dst = rhos[j].at[pl.ds(NXL + HALO if dx < 0 else 0, HALO)]
        else:
            s = 0 if dy < 0 else 1
            x0, n, to = {-1: (0, 8, 40), 0: (0, NXL, 8), 1: (NXL - 8, 8, 0)}[dx]
            src = ss.at[j, s, :, pl.ds(x0, n), :]
            dst = sr.at[j, 1 - s, :, pl.ds(to, n), :]
        return pltpu.make_async_remote_copy(
            src_ref=src, dst_ref=dst, send_sem=sx_sem.at[j, i], recv_sem=rx_sem.at[j, i],
            device_id=side_dev(dx, dy), device_id_type=MESH,
        )

    along_x = [i for i, (dx, dy) in enumerate(SIDES) if dy == 0]
    along_y = [i for i, (dx, dy) in enumerate(SIDES) if dx == 0]
    corners = [i for i, (dx, dy) in enumerate(SIDES) if dx and dy]

    def send(j, which):
        for i in which:
            pl.when(exists(*SIDES[i]))(lambda i=i: face(j, i).start())

    def receive(j):
        for i, (dx, dy) in enumerate(SIDES):
            pl.when(exists(-dx, -dy))(lambda i=i: face(j, i).wait_recv())

    for i in corners + along_x + along_y:
        pl.when(exists(*SIDES[i]))(lambda i=i: block_copy(i).start())
    send(0, along_x + corners + along_y)
    line_inverses(kpad[...], (w0, w1))

    def line_pass0(i, carry):
        for x8 in range(ROWS):
            x = i * ROWS + x8
            e0 = split_mm(rho0[x + HALO].reshape(128, 128), w0[...])
            put(e0b, cb0, HALO, x, 0, e0[:NY2])
            put(e0b, cb0, HALO, x, 1, e0[NY2:])
        return carry

    lax.fori_loop(0, NXL // ROWS, line_pass0, 0)

    for i in range(8):
        dx, dy = SIDES[i]
        pl.when(exists(-dx, -dy))(lambda i=i: block_copy(i).wait_recv())

    low_half = lax.broadcasted_iota(jnp.int32, (96, 128), 1) < 64

    def around(rows):
        def column(dy):
            parts = []
            for dx in (-1, 0, 1):
                if (dx, dy) == (0, 0):
                    parts.append(blk[rows, :])
                else:
                    parts.append(nbr[SIDES.index((-dx, -dy)), rows, :])
            return roll(jnp.concatenate(parts, axis=0), 64, 1)

        left, mid, right = column(-1), column(0), column(1)
        return jnp.concatenate(
            [jnp.where(low_half, left, mid), jnp.where(low_half, mid, right)], axis=1
        )

    def local(v):
        a, b = roll(v[:, 0:128], 64, 1), roll(v[:, 128:256], 64, 1)
        return jnp.where(low_half[: v.shape[0]], a, b)

    moves = ((-1, 0), (1, 0), (-1, 1), (1, 1))
    mask2 = around(pl.ds(0, NXL))
    m2[...] = mask2
    bars[0] = around(pl.ds(NXL, NXL))
    open_sides = jnp.zeros((96, 256), F32)
    for i, (s, axis) in enumerate(moves):
        beside = roll(mask2, s, axis)
        mn[i] = beside
        open_sides = open_sides + beside
    own2 = mask2 * (4.0 - open_sides)
    to_columns(local(mask2[24:72]))
    expand(m3, 6, 8, -6)
    expand(m3, 40, 42, -6)
    to_columns(local(own2[24:72]))
    expand(q3, 6, 42, -6)
    for a in range(2):
        for s, at in ((0, 63 - a), (1, 192 + a)):
            sm[s, a] = jnp.broadcast_to(mask2[24:72, at : at + 1], (48, 128))
            sq[s, a] = jnp.broadcast_to(own2[24:72, at : at + 1], (48, 128))

    xi = lax.broadcasted_iota(jnp.int32, (96, 256), 0) + (gx * NXL - 32)
    yi = lax.broadcasted_iota(jnp.int32, (96, 256), 1) + (gy * 128 - 64)
    inside = (xi >= 0) & (xi < nx * NXL) & (yi >= 0) & (yi < ny * 128)
    dom = jnp.where(inside, 1.0, 0.0)

    even_x = lax.rem(lax.broadcasted_iota(jnp.int32, (96, 256), 0), 2) == 0
    even_y = lax.rem(lax.broadcasted_iota(jnp.int32, (96, 256), 1), 2) == 0
    even_s = lax.rem(lax.broadcasted_iota(jnp.int32, (48, 128), 0), 2) == 0

    def flow(v):
        total = None
        for i, (s, axis) in enumerate(moves):
            term = mn[i] * (roll(v, s, axis) - v)
            total = term if total is None else total + term
        return total

    def mean_step(j):
        m = m2[...]
        e0 = bars[j] * (1.0 / 4.1)
        t = 4.0 * e0 + flow(e0)
        t1 = m * t
        t1 = t1 + jnp.where(even_x, roll(t1, -1, 0), roll(t1, 1, 0))
        t1 = t1 + jnp.where(even_y, roll(t1, -1, 1), roll(t1, 1, 1))
        e1 = t1 * (1.0 / 4.4)
        c = (0.8 / 4.4) * t1
        for _ in range(SWEEPS - 1):
            beside = (roll(c, 2, 0) + roll(c, -2, 0)) + (roll(c, 2, 1) + roll(c, -2, 1))
            c = dom * (c + 0.8 * (t1 - (4.4 * c - beside)) / 4.4)
        f = e1 + c
        rem = m * (t + flow(f) + (e1 - 0.25 * t1) - 0.1 * c)
        d = rem * (1.0 / 4.1)
        ybars[j] = e0 + m * f + d
        bars[j + 1] = m * (4.0 * d + flow(d))

    def insert(dst, src, shift, x):
        dst[x + shift, 1, 7:8, :] = src[0, pl.ds(x + 8, 1), :]
        dst[x + shift, 0, 72:73, :] = src[1, pl.ds(x + 8, 1), :]

    def stencil_rows(src, shift, x0, count, less=None):
        out = {}
        for h in range(2):
            y0 = 8 + H * h
            held = {}

            def centre(x, b):
                if (x, b) not in held:
                    held[x, b] = src[x0 + x + shift, b, y0 : y0 + H, :]
                return held[x, b]

            for x in range(count):
                minus = None if less is None else less(x, h)
                for b in range(2):
                    at = y0 - 1 if b == 0 else y0 + 1
                    beside = centre(x, 1 - b) + src[x0 + x + shift, 1 - b, at : at + H, :]
                    beside = beside + (centre(x - 1, b) + centre(x + 1, b))
                    if minus is not None:
                        beside = beside - minus
                    q = q3[x0 + x + 2, b, H * h : H * h + H, :]
                    m = m3[x0 + x + 2, b, H * h : H * h + H, :]
                    out[x, h, b] = q * centre(x, b) + m * beside
        return out

    def strip_beside(v):
        return roll(v, 1, 0) + roll(v, -1, 0)

    def halo_lines(j):
        for x in (-3, -2, -1, 32, 33, 34):
            e0 = split_mm(rhos[j][x + HALO].reshape(128, 128), w0[...])
            put(e0b, cb0, HALO, x, 0, e0[:NY2])
            put(e0b, cb0, HALO, x, 1, e0[NY2:])
        se0[...] = split_mm(sr[j].reshape(288, 128), w0[...]).reshape(2, 3, 48, 128)

    def strip_correct():
        t1 = []
        for s in range(2):
            near, mid, far = se0[s, 0], se0[s, 1], se0[s, 2]
            t = sq[s, 0] * near + sm[s, 0] * (cb0[s] + mid + strip_beside(near))
            t = t + sq[s, 1] * mid + sm[s, 1] * (near + far + strip_beside(mid))
            t1.append(t + jnp.where(even_s, roll(t, -1, 0), roll(t, 1, 0)))
        t1 = jnp.concatenate(t1, axis=0)
        e1 = split_mm(t1, w1[...])
        h1 = 0.25 * t1 + 3.0 * e1
        for s in range(2):
            part = e1[48 * s : 48 * s + 48]
            for a in range(2):
                se[s, a] = se0[s, a] + sm[s, a] * part
            sd[s] = h1[48 * s : 48 * s + 48]

    def strip_smooth():
        rem = []
        for s in range(2):
            near, far = se[s, 0], se[s, 1]
            rem.append(sq[s, 0] * near + sm[s, 0] * (cb[s] + far + strip_beside(near) - sd[s]))
        sd[...] = split_mm(jnp.concatenate(rem, axis=0), w0[...]).reshape(2, 48, 128)

    def correct_pass():
        def body(i, carry):
            x0 = i * 12 - 2
            for x in range(12):
                insert(e0b, se0.at[:, 0], HALO, x0 + x)
            t = stencil_rows(e0b, HALO, x0, 12)
            keys = [(k, h) for h in range(2) for k in range(6)]
            t1 = jnp.concatenate(
                [
                    (t[2 * k, h, 0] + t[2 * k, h, 1]) + (t[2 * k + 1, h, 0] + t[2 * k + 1, h, 1])
                    for k, h in keys
                ],
                axis=0,
            )
            e1 = split_mm(t1, w1[...])
            h1 = 0.25 * t1 + 3.0 * e1
            for n, (k, h) in enumerate(keys):
                part = e1[n * H : n * H + H]
                h1s[i * 6 + k, h * H : h * H + H, :] = h1[n * H : n * H + H]
                for x in (2 * k, 2 * k + 1):
                    for b in range(2):
                        m = m3[x0 + x + 2, b, h * H : h * H + H, :]
                        e0 = e0b[x0 + x + HALO, b, 8 + h * H : 8 + h * H + H, :]
                        put(eb, cb, HALO, x0 + x, b, e0 + m * part, h)
            return carry

        lax.fori_loop(0, 3, body, 0)

    def smooth_rows(x0, count, half0):
        for x in range(count):
            insert(eb, se.at[:, 0], HALO, x0 + x)
        rem = stencil_rows(
            eb, HALO, x0, count,
            lambda x, h: h1s[half0 + x // 2 + 1, h * H : h * H + H, :],
        )
        d = split_mm(jnp.concatenate(list(rem.values()), axis=0), w0[...])
        return [(key, d[n * H : n * H + H]) for n, key in enumerate(rem)]

    def smooth_pass(j):
        for x0, half0 in ((-1, -1), (NXL, NXL // 2)):
            for (x, h, b), d in smooth_rows(x0, 1, half0):
                put(db, None, 1, x0 + x, b, d, h)

        def body(i, acc):
            x0 = i * ROWS
            for (x, h, b), d in smooth_rows(x0, ROWS, i * (ROWS // 2)):
                y = eb[x0 + x + HALO, b, 8 + h * H : 8 + h * H + H, :] + d
                put(db, None, 1, x0 + x, b, d, h)
                ys[j][x0 + x, b, h * H : h * H + H, :] = y
                acc = acc + tile_sum(rhos[j][x0 + x + HALO, b, h * H : h * H + H, :] * y)
            return acc

        return lax.fori_loop(0, NXL // ROWS, body, jnp.zeros((8, 128), F32))

    def next_pass(j):
        shift = HALO if j + 1 < ITERS else 0

        def rows(i, acc):
            x0 = i * ROWS
            for x in range(ROWS):
                insert(db, sd, 1, x0 + x)
            new = stencil_rows(db, 1, x0, ROWS)
            for (x, h, b), v in new.items():
                rhos[j + 1][x0 + x + shift, b, h * H : h * H + H, :] = v
                acc = acc + tile_sum(v * ys[j][x0 + x, b, h * H : h * H + H, :])
                if j + 1 < ITERS:
                    put_sides(ss.at[j + 1], x0 + x, b, v, h)
            if j + 1 < ITERS:
                e0 = split_mm(jnp.concatenate(list(new.values()), axis=0), w0[...])
                for n, (x, h, b) in enumerate(new):
                    put(e0b, cb0, HALO, x0 + x, b, e0[n * H : n * H + H], h)
            return acc

        last = NXL // ROWS - 1
        acc = lax.fori_loop(0, 2, lambda i, a: rows(i * last, a), jnp.zeros((8, 128), F32))
        if j + 1 < ITERS:
            send(j + 1, along_x + corners)
        acc = lax.fori_loop(1, last, rows, acc)
        if j + 1 < ITERS:
            send(j + 1, along_y)
        return acc

    for j in range(ITERS):
        receive(j)
        halo_lines(j)
        strip_correct()
        correct_pass()
        strip_smooth()
        acc = smooth_pass(j)
        nus[2 * j] = acc + nu0 if j == 0 else acc
        nus[2 * j + 1] = next_pass(j)
        if j == 0:
            mean_step(0)
            mean_step(1)
        if j == 1:
            mean_step(2)

    rows = lax.broadcasted_iota(jnp.int32, (8, 128), 0)
    part = jnp.zeros((8, 128), F32)
    here = pl.ds(32, NXL)
    for n in range(2 * ITERS):
        rho, y = local(bars[(n + 1) // 2, here]), local(ybars[n // 2, here])
        v = nus[n] + 128.0 * jnp.sum((rho * y).reshape(4, 8, 128), axis=0)
        part = part + jnp.where(rows == n, jnp.sum(v, axis=0, keepdims=True), 0.0)
    total, copies = part, []
    for n, devs in enumerate(phases):
        red, base = reds[n], len(copies)
        red[0] = total
        for i, dev in enumerate(devs):
            copy = pltpu.make_async_remote_copy(
                src_ref=red.at[0], dst_ref=red.at[i + 1], send_sem=ss_sem.at[base + i],
                recv_sem=rs_sem.at[base + i], device_id=dev, device_id_type=MESH,
            )
            copy.start()
            copies.append(copy)
        for copy in copies[base:]:
            copy.wait_recv()
        total = jnp.sum(red[...], axis=0)
    total = jnp.broadcast_to(jnp.sum(total, axis=1, keepdims=True), (8, 128))
    nu = [total[n : n + 1] for n in range(2 * ITERS)]

    h00, h10, h20 = nu[0] - nu[1], nu[1] - nu[2], nu[2] - nu[3]
    h11, h21, h22 = nu[2] - nu[3], nu[3] - nu[4], nu[4] - nu[5]
    l10, l20 = h10 / h00, h20 / h00
    d1, s21 = h11 - l10 * h10, h21 - l10 * h20
    l21 = s21 / d1
    d2 = h22 - l20 * h20 - l21 * s21
    b1 = nu[1] - l10 * nu[0]
    b2 = nu[2] - l20 * nu[0] - l21 * b1
    c2 = b2 / d2
    c1 = b1 / d1 - l21 * c2
    c0 = nu[0] / h00 - l10 * c1 - l20 * c2
    a0, a1, a2 = 1.0 - c0, c0 - c1, c1 - c2

    xbar = c0 * local(ybars[0, here]) + c1 * local(ybars[1, here]) + c2 * local(ybars[2, here])
    rbar = a1 * local(bars[1, here]) + a2 * local(bars[2, here]) + c2 * local(bars[3, here])
    to_columns(xbar)
    xcols = [tmat[pl.ds(b, NY2, stride=2), :] for b in range(2)]
    to_columns(rbar)
    rcols = [tmat[pl.ds(b, NY2, stride=2), :] for b in range(2)]

    for g in range(4):
        for x in range(8 * g, 8 * g + 8):
            for b in range(2):
                v = inp[x, pl.ds(b, NY2, stride=2), :]
                m = m3[x + 2, b]
                ox = c0 * y0[x, b] + c1 * y1[x, b] + c2 * y2[x, b]
                ox = ox + c0 * ((1.0 - m) * v) + xcols[b][:, x : x + 1]
                orr = a0 * v + a1 * rho1[x + HALO, b] + a2 * rho2[x + HALO, b] + c2 * rho3[x, b]
                orr = orr + rcols[b][:, x : x + 1]
                x_ref[x, pl.ds(b, NY2, stride=2), :] = ox
                r_ref[x, pl.ds(b, NY2, stride=2), :] = orr

    for i in range(8):
        pl.when(exists(*SIDES[i]))(lambda i=i: block_copy(i).wait_send())
        for j in range(ITERS):
            pl.when(exists(*SIDES[i]))(lambda i=i, j=j: face(j, i).wait_send())
    for copy in copies:
        copy.wait_send()


def shards(nx, ny, right_side, sea_mask, vertical_coupling):
    vmem = pltpu.VMEM
    sizes = {"x": nx // 8, "y": 4, "c": 2, "z": ny}
    counts = [math.prod(sizes[axis] for axis in axes) for axes in PHASES]
    counts = counts + [1] * (3 - len(counts))
    out = pltpu.VMEM(right_side.shape, F32)
    return pl.pallas_call(
        functools.partial(kernel, nx, ny),
        out_shape=(out, out),
        in_specs=[
            pl.BlockSpec(memory_space=pltpu.HBM),
            pl.BlockSpec(memory_space=pltpu.HBM),
            pl.BlockSpec(memory_space=pltpu.HBM),
        ],
        out_specs=(pl.BlockSpec(memory_space=vmem), pl.BlockSpec(memory_space=vmem)),
        scratch_shapes=[
            vmem((NXL, 128), jnp.int32),
            vmem((1, 127), F32),
            vmem((NXL, 128, 128), F32),
            vmem((NXL + 2 * HALO, 2, NY2, 128), F32),
            vmem((NXL + 2 * HALO, 2, NY2, 128), F32),
            vmem((NXL + 2 * HALO, 2, NY2, 128), F32),
            vmem((NXL, 2, NY2, 128), F32),
            vmem((NXL, 2, NY2, 128), F32),
            vmem((NXL, 2, NY2, 128), F32),
            vmem((NXL, 2, NY2, 128), F32),
            vmem((NXL + 2 * HALO, 2, 80, 128), F32),
            vmem((NXL + 2 * HALO, 2, 80, 128), F32),
            vmem((NXL + 2, 2, 80, 128), F32),
            vmem((NXL // 2 + 2, NY2, 128), F32),
            vmem((NXL + 4, 2, NY2, 128), F32),
            vmem((NXL + 4, 2, NY2, 128), F32),
            vmem((ITERS, 2, 3, 48, 128), F32),
            vmem((ITERS, 2, 3, NXL, 128), F32),
            vmem((2, 3, 48, 128), F32),
            vmem((2, 2, 48, 128), F32),
            vmem((2, 48, 128), F32),
            vmem((2, 48, 128), F32),
            vmem((2, 48, 128), F32),
            vmem((2, 2, 48, 128), F32),
            vmem((2, 2, 48, 128), F32),
            vmem((256, 256), BF16),
            vmem((256, 256), BF16),
            vmem((1, 128), F32),
            vmem((2 * NXL, 128), F32),
            vmem((8, 2 * NXL, 128), F32),
            vmem((128, 128), F32),
            vmem((4, 96, 256), F32),
            vmem((96, 256), F32),
            vmem((ITERS + 1, 96, 256), F32),
            vmem((ITERS, 96, 256), F32),
            vmem((2 * ITERS, 8, 128), F32),
            *[vmem((n, 8, 128), F32) for n in counts],
            pltpu.SemaphoreType.DMA((3,)),
            pltpu.SemaphoreType.DMA((ITERS, 8)),
            pltpu.SemaphoreType.DMA((ITERS, 8)),
            pltpu.SemaphoreType.DMA((8,)),
            pltpu.SemaphoreType.DMA((8,)),
            pltpu.SemaphoreType.DMA((sum(counts),)),
            pltpu.SemaphoreType.DMA((sum(counts),)),
        ],
        compiler_params=pltpu.CompilerParams(
            collective_id=0, has_side_effects=True, vmem_limit_bytes=56 * 1024 * 1024
        ),
    )(right_side, sea_mask, vertical_coupling.reshape(1, -1))


def solution(mesh):
    nx, ny = mesh.shape["gx"], mesh.shape["gy"]
    return jax.shard_map(
        functools.partial(shards, nx, ny),
        mesh=mesh,
        in_specs=(P("gx", "gy", None), P("gx", "gy"), P()),
        out_specs=(P("gx", "gy", None), P("gx", "gy", None)),
        check_vma=False,
    )
```

```python
import functools
import itertools
import math

import jax
import jax.numpy as jnp
from jax import lax
from jax.experimental import pallas as pl
from jax.experimental.pallas import tpu as pltpu
from jax.sharding import PartitionSpec as P


ITERS = 3
SWEEPS = 4
F32 = jnp.float32
BF16 = jnp.bfloat16
MESH = pl.DeviceIdType.MESH
NXL, NY2, NZ = 32, 64, 128
ROWS = 8
HALO = 3
EDGE = 4
HALVES = ((0, 32), (32, 32))
INNER = ((8, 24), (32, 24))
OUTER = ((0, 8), (56, 8))
PHASES = ("cz", "xy")
SIDES = [(dx, dy) for dx in (-1, 0, 1) for dy in (-1, 0, 1) if (dx, dy) != (0, 0)]


def split_mm(v, w):
    high = v.astype(BF16)
    low = (v - high.astype(F32)).astype(BF16)
    o = jnp.dot(jnp.concatenate([high, low], axis=1), w, preferred_element_type=F32)
    return o[:, :128] + o[:, 128:]


def roll(v, shift, axis):
    return pltpu.roll(v, shift % v.shape[axis], axis)


def line_inverses(coupling, w_refs):
    lane = lax.broadcasted_iota(jnp.int32, (8, 128), 1)
    row = lax.broadcasted_iota(jnp.int32, (8, 128), 0)
    up = jnp.broadcast_to(coupling, (8, 128))
    lo = roll(up, 1, 1)
    factor = jnp.where(row == 0, 1.0, 4.0)
    diag = jnp.where(row == 0, 4.1, 4.4) + factor * (up + lo)
    off_up = factor * up
    off_lo = factor * lo

    def pivots(off, step):
        a, b = diag, -off * off
        c, d = jnp.ones_like(a), jnp.zeros_like(a)
        s = 1
        while s < 128:
            inside = (lane >= s) if step > 0 else (lane < 128 - s)
            ra = jnp.where(inside, roll(a, step * s, 1), 1.0)
            rb = jnp.where(inside, roll(b, step * s, 1), 0.0)
            rc = jnp.where(inside, roll(c, step * s, 1), 0.0)
            rd = jnp.where(inside, roll(d, step * s, 1), 1.0)
            na, nb = a * ra + b * rc, a * rb + b * rd
            nc, nd = c * ra + d * rc, c * rb + d * rd
            inv = 1.0 / na
            a, b, c, d = jnp.ones_like(a), nb * inv, nc * inv, nd * inv
            s *= 2
        return 1.0 / c

    fore = pivots(off_lo, 1)
    back = pivots(off_up, -1)
    main = 1.0 / (fore + back - diag)
    ratio = jnp.where(lane < 127, jnp.log(jnp.maximum(off_up, 1e-30) / fore), 0.0)
    total = jnp.where(lane >= 1, roll(ratio, 1, 1), 0.0)
    s = 1
    while s < 128:
        total = total + jnp.where(lane >= s, roll(total, s, 1), 0.0)
        s *= 2

    r = lax.broadcasted_iota(jnp.int32, (128, 128), 0)
    c = lax.broadcasted_iota(jnp.int32, (128, 128), 1)
    for i, w_ref in enumerate(w_refs):
        def wide(v):
            return jnp.broadcast_to(v[i : i + 1], (128, 128))

        g_row, t_row = wide(main), wide(total)
        g_col, t_col = g_row.T, t_row.T
        g = jnp.where(r <= c, g_row, g_col) * jnp.exp(-jnp.abs(t_row - t_col))
        a_col, u_col = wide(diag).T, wide(off_up).T
        l_col = wide(off_lo).T
        tg = a_col * g - u_col * roll(g, -1, 0) - l_col * roll(g, 1, 0)
        rest = jnp.where(r == c, 1.0, 0.0) - tg
        g = g + jnp.dot(g.astype(BF16), rest.astype(BF16), preferred_element_type=F32)
        high = g.astype(BF16)
        low = (g - high.astype(F32)).astype(BF16)
        both = jnp.concatenate([high, low], axis=1)
        w_ref[...] = jnp.concatenate([both, both], axis=0)


def kernel(
    nx, ny, rhs_ref, mask_hbm, coup_hbm, x_ref, r_ref,
    mask_ref, coup_ref, inp, rho0, rho1, rho2, rho3, y0, y1, y2, e0b, eb, db, h1s, m3, q3,
    sr, ss, se0, se, sd, cb0, cb, sm, sq, w0, w1, kpad,
    blk, nbr, tmat, mn, m2, bars, ybars, nus, dots, cols, red0, red1, red2,
    in_sem, sx_sem, rx_sem, sb_sem, rb_sem, ss_sem, rs_sem,
):
    gx, gy = lax.axis_index("gx"), lax.axis_index("gy")
    reds = (red0, red1, red2)
    rhos, ys = (rho0, rho1, rho2, rho3), (y0, y1, y2)

    sizes = {"x": nx // 8, "y": 4, "c": 2, "z": ny}
    place = {"x": lax.div(gx, 8), "y": lax.rem(lax.div(gx, 2), 4), "c": lax.rem(gx, 2), "z": gy}

    def partners(axes):
        devs = []
        for steps in itertools.product(*(range(sizes[axis]) for axis in axes)):
            if any(steps):
                at = dict(place)
                for axis, step in zip(axes, steps):
                    at[axis] = lax.rem(place[axis] + step, sizes[axis])
                devs.append((at["x"] * 8 + at["y"] * 2 + at["c"], at["z"]))
        return devs

    phases = [partners(axes) for axes in PHASES]

    def side_dev(dx, dy):
        return (lax.rem(gx + dx + nx, nx), lax.rem(gy + dy + ny, ny))

    small = [
        pltpu.make_async_copy(coup_hbm, coup_ref, in_sem.at[0]),
        pltpu.make_async_copy(mask_hbm, mask_ref, in_sem.at[1]),
    ]
    load = pltpu.make_async_copy(rhs_ref, inp, in_sem.at[2])
    for copy in small:
        copy.start()
    load.start()

    def clear(x, carry):
        zero = jnp.zeros((2, NY2, 128), F32)
        for rho in (rho0, rho1, rho2):
            rho[x] = zero
            rho[x + NXL + HALO] = zero
        return carry

    lax.fori_loop(0, HALO, clear, 0)
    sr[...] = jnp.zeros(sr.shape, F32)
    nbr[...] = jnp.zeros(nbr.shape, F32)
    cb0[...] = jnp.zeros(cb0.shape, F32)
    cb[...] = jnp.zeros(cb.shape, F32)

    barrier = pltpu.get_barrier_semaphore()
    for dx, dy in SIDES:
        pl.semaphore_signal(barrier, inc=1, device_id=side_dev(dx, dy), device_id_type=MESH)
    for dev in sum(phases, []):
        pl.semaphore_signal(barrier, inc=1, device_id=dev, device_id_type=MESH)

    for copy in small:
        copy.wait()
    kpad[...] = jnp.zeros((1, 128), F32)
    kpad[:, 0:127] = coup_ref[...]

    lane = lax.broadcasted_iota(jnp.int32, (NY2, 128), 1)

    def to_columns(v):
        tmat[...] = jnp.concatenate([v, jnp.zeros((128 - v.shape[0], 128), F32)], axis=0).T

    def expand(dst, start, stop, shift):
        for b in range(2):
            col = tmat[pl.ds(b, NY2, stride=2), :]
            for x in range(start, stop):
                dst[x + shift, b] = jnp.broadcast_to(col[:, x : x + 1], (NY2, 128))

    mask = mask_ref[...].astype(F32)
    blk[0:NXL, :] = mask
    to_columns(mask)
    expand(m3, 0, NXL, 2)

    def put_sides(dst, x, b, v, y0=0):
        n = v.shape[0]
        for half, d, row in (
            ((0, 0, 0), (0, 2, 1), (1, 1, n - 1)) if b == 0 else ((0, 1, 0), (1, 0, n - 1), (1, 2, n - 2))
        ):
            if y0 == 0 if half == 0 else y0 + n == NY2:
                dst[half, d, pl.ds(x, 1), :] = v[row : row + 1]

    def put(dst, edge, shift, x, b, v, y0=0):
        n = v.shape[0]
        dst[x + shift, b, 8 + y0 : 8 + y0 + n, :] = v
        if edge is not None and (y0 == 0 if b == 0 else y0 + n == NY2):
            edge[b, pl.ds(x + 8, 1), :] = v[0:1] if b == 0 else v[n - 1 : n]

    def tile_sum(v):
        return jnp.sum(v.reshape(-1, 8, 128), axis=0)

    load.wait()

    def start_pass(i, carry):
        acc, means = carry[0], list(carry[1:])
        for x, b in [(i * 4 + k, b) for k in range(4) for b in range(2)]:
            v = inp[x, pl.ds(b, NY2, stride=2), :]
            m = m3[x + 2, b]
            mean = jnp.sum(v, axis=1, keepdims=True) * (1.0 / NZ)
            means[b] = jnp.where(lane == x, mean, means[b])
            dev = m * (v - mean)
            rho0[x + HALO, b] = dev
            put_sides(ss.at[0], x, b, dev)
            land = (1.0 - m) * v
            acc = acc + tile_sum(land * land)
        return (acc, *means)

    zero = jnp.zeros((NY2, 128), F32)
    nu0, mean0, mean1 = lax.fori_loop(0, NXL // 4, start_pass, (jnp.zeros((8, 128), F32), zero, zero))
    tmat[pl.ds(0, NY2, stride=2), :] = mean0
    tmat[pl.ds(1, NY2, stride=2), :] = mean1
    blk[NXL : 2 * NXL, :] = mask * tmat[...].T[0:NXL]

    pl.semaphore_wait(barrier, len(SIDES) + sum(map(len, phases)))

    def exists(dx, dy):
        ok = None
        for pos, d, n in ((gx, dx, nx), (gy, dy, ny)):
            if d:
                here = (pos + d >= 0) & (pos + d < n)
                ok = here if ok is None else ok & here
        return ok

    def block_copy(i):
        return pltpu.make_async_remote_copy(
            src_ref=blk, dst_ref=nbr.at[i], send_sem=sb_sem.at[i], recv_sem=rb_sem.at[i],
            device_id=side_dev(*SIDES[i]), device_id_type=MESH,
        )

    def face(j, i):
        dx, dy = SIDES[i]
        if dy == 0:
            src = rhos[j].at[pl.ds(HALO if dx < 0 else NXL, HALO)]
            dst = rhos[j].at[pl.ds(NXL + HALO if dx < 0 else 0, HALO)]
        else:
            s = 0 if dy < 0 else 1
            x0, n, to = {-1: (0, 8, 40), 0: (0, NXL, 8), 1: (NXL - 8, 8, 0)}[dx]
            src = ss.at[j, s, :, pl.ds(x0, n), :]
            dst = sr.at[j, 1 - s, :, pl.ds(to, n), :]
        return pltpu.make_async_remote_copy(
            src_ref=src, dst_ref=dst, send_sem=sx_sem.at[j, i], recv_sem=rx_sem.at[j, i],
            device_id=side_dev(dx, dy), device_id_type=MESH,
        )

    along_x = [i for i, (dx, dy) in enumerate(SIDES) if dy == 0]
    along_y = [i for i, (dx, dy) in enumerate(SIDES) if dx == 0]
    corners = [i for i, (dx, dy) in enumerate(SIDES) if dx and dy]

    def send(j, which):
        for i in which:
            pl.when(exists(*SIDES[i]))(lambda i=i: face(j, i).start())

    def receive(j):
        for i, (dx, dy) in enumerate(SIDES):
            pl.when(exists(-dx, -dy))(lambda i=i: face(j, i).wait_recv())

    for i in corners + along_x + along_y:
        pl.when(exists(*SIDES[i]))(lambda i=i: block_copy(i).start())
    send(0, along_x + corners + along_y)
    line_inverses(kpad[...], (w0, w1))

    def line_pass(j):
        def body(i, carry):
            for x8 in range(ROWS):
                x = i * ROWS + x8
                e0 = split_mm(rhos[j][x + HALO].reshape(128, 128), w0[...])
                put(e0b, cb0, HALO, x, 0, e0[:NY2])
                put(e0b, cb0, HALO, x, 1, e0[NY2:])
            return carry

        lax.fori_loop(0, NXL // ROWS, body, 0)

    line_pass(0)

    for i in range(8):
        dx, dy = SIDES[i]
        pl.when(exists(-dx, -dy))(lambda i=i: block_copy(i).wait_recv())

    low_half = lax.broadcasted_iota(jnp.int32, (96, 128), 1) < 64

    def around(rows):
        def column(dy):
            parts = []
            for dx in (-1, 0, 1):
                if (dx, dy) == (0, 0):
                    parts.append(blk[rows, :])
                else:
                    parts.append(nbr[SIDES.index((-dx, -dy)), rows, :])
            return roll(jnp.concatenate(parts, axis=0), 64, 1)

        left, mid, right = column(-1), column(0), column(1)
        return jnp.concatenate(
            [jnp.where(low_half, left, mid), jnp.where(low_half, mid, right)], axis=1
        )

    def local(v):
        a, b = roll(v[:, 0:128], 64, 1), roll(v[:, 128:256], 64, 1)
        return jnp.where(low_half[: v.shape[0]], a, b)

    moves = ((-1, 0), (1, 0), (-1, 1), (1, 1))
    mask2 = around(pl.ds(0, NXL))
    m2[...] = mask2
    bars[0] = around(pl.ds(NXL, NXL))
    open_sides = jnp.zeros((96, 256), F32)
    for i, (s, axis) in enumerate(moves):
        beside = roll(mask2, s, axis)
        mn[i] = beside
        open_sides = open_sides + beside
    own2 = mask2 * (4.0 - open_sides)
    to_columns(local(mask2[24:72]))
    expand(m3, 6, 8, -6)
    expand(m3, 40, 42, -6)
    to_columns(local(own2[24:72]))
    expand(q3, 6, 42, -6)
    for a in range(2):
        for s, at in ((0, 63 - a), (1, 192 + a)):
            sm[s, a] = jnp.broadcast_to(mask2[24:72, at : at + 1], (48, 128))
            sq[s, a] = jnp.broadcast_to(own2[24:72, at : at + 1], (48, 128))

    xi = lax.broadcasted_iota(jnp.int32, (96, 256), 0) + (gx * NXL - 32)
    yi = lax.broadcasted_iota(jnp.int32, (96, 256), 1) + (gy * 128 - 64)
    inside = (xi >= 0) & (xi < nx * NXL) & (yi >= 0) & (yi < ny * 128)
    dom = jnp.where(inside, 1.0, 0.0)

    even_x = lax.rem(lax.broadcasted_iota(jnp.int32, (96, 256), 0), 2) == 0
    even_y = lax.rem(lax.broadcasted_iota(jnp.int32, (96, 256), 1), 2) == 0
    even_s = lax.rem(lax.broadcasted_iota(jnp.int32, (48, 128), 0), 2) == 0

    def flow(v):
        total = None
        for i, (s, axis) in enumerate(moves):
            term = mn[i] * (roll(v, s, axis) - v)
            total = term if total is None else total + term
        return total

    def mean_step(j):
        m = m2[...]
        e0 = bars[j] * (1.0 / 4.1)
        t = 4.0 * e0 + flow(e0)
        t1 = m * t
        t1 = t1 + jnp.where(even_x, roll(t1, -1, 0), roll(t1, 1, 0))
        t1 = t1 + jnp.where(even_y, roll(t1, -1, 1), roll(t1, 1, 1))
        e1 = t1 * (1.0 / 4.4)
        c = (0.8 / 4.4) * t1
        for _ in range(SWEEPS - 1):
            beside = (roll(c, 2, 0) + roll(c, -2, 0)) + (roll(c, 2, 1) + roll(c, -2, 1))
            c = dom * (c + 0.8 * (t1 - (4.4 * c - beside)) / 4.4)
        f = e1 + c
        rem = m * (t + flow(f) + (e1 - 0.25 * t1) - 0.1 * c)
        d = rem * (1.0 / 4.1)
        ybars[j] = e0 + m * f + d
        bars[j + 1] = m * (4.0 * d + flow(d))

    def insert(dst, src, shift, x):
        dst[x + shift, 1, 7:8, :] = src[0, pl.ds(x + 8, 1), :]
        dst[x + shift, 0, 72:73, :] = src[1, pl.ds(x + 8, 1), :]

    def stencil_rows(src, shift, x0, count, parts=HALVES, less=None):
        out = {}
        for y0, n in parts:
            held = {}

            def centre(x, b):
                if (x, b) not in held:
                    held[x, b] = src[x0 + x + shift, b, 8 + y0 : 8 + y0 + n, :]
                return held[x, b]

            for x in range(count):
                minus = None if less is None else less(x, y0, n)
                for b in range(2):
                    at = 7 + y0 if b == 0 else 9 + y0
                    beside = centre(x, 1 - b) + src[x0 + x + shift, 1 - b, at : at + n, :]
                    beside = beside + (centre(x - 1, b) + centre(x + 1, b))
                    if minus is not None:
                        beside = beside - minus
                    q = q3[x0 + x + 2, b, y0 : y0 + n, :]
                    m = m3[x0 + x + 2, b, y0 : y0 + n, :]
                    out[x, y0, b] = q * centre(x, b) + m * beside
        return out

    def strip_beside(v):
        return roll(v, 1, 0) + roll(v, -1, 0)

    def halo_lines(j):
        for x in (-3, -2, -1, 32, 33, 34):
            e0 = split_mm(rhos[j][x + HALO].reshape(128, 128), w0[...])
            put(e0b, cb0, HALO, x, 0, e0[:NY2])
            put(e0b, cb0, HALO, x, 1, e0[NY2:])
        se0[...] = split_mm(sr[j].reshape(288, 128), w0[...]).reshape(2, 3, 48, 128)

    def strip_correct():
        t1 = []
        for s in range(2):
            near, mid, far = se0[s, 0], se0[s, 1], se0[s, 2]
            t = sq[s, 0] * near + sm[s, 0] * (cb0[s] + mid + strip_beside(near))
            t = t + sq[s, 1] * mid + sm[s, 1] * (near + far + strip_beside(mid))
            t1.append(t + jnp.where(even_s, roll(t, -1, 0), roll(t, 1, 0)))
        t1 = jnp.concatenate(t1, axis=0)
        e1 = split_mm(t1, w1[...])
        h1 = 0.25 * t1 + 3.0 * e1
        for s in range(2):
            part = e1[48 * s : 48 * s + 48]
            for a in range(2):
                se[s, a] = se0[s, a] + sm[s, a] * part
            sd[s] = h1[48 * s : 48 * s + 48]

    def strip_smooth():
        rem = []
        for s in range(2):
            near, far = se[s, 0], se[s, 1]
            rem.append(sq[s, 0] * near + sm[s, 0] * (cb[s] + far + strip_beside(near) - sd[s]))
        sd[...] = split_mm(jnp.concatenate(rem, axis=0), w0[...]).reshape(2, 48, 128)

    def correct_block(first, count, parts):
        x0 = 2 * first
        t = stencil_rows(e0b, HALO, x0, 2 * count, parts)
        keys = [(k, y0, n) for y0, n in parts for k in range(count)]
        t1 = jnp.concatenate(
            [
                (t[2 * k, y0, 0] + t[2 * k, y0, 1]) + (t[2 * k + 1, y0, 0] + t[2 * k + 1, y0, 1])
                for k, y0, n in keys
            ],
            axis=0,
        )
        e1 = split_mm(t1, w1[...])
        h1 = 0.25 * t1 + 3.0 * e1
        at = 0
        for k, y0, n in keys:
            part = e1[at : at + n]
            h1s[first + k + 1, y0 : y0 + n, :] = h1[at : at + n]
            at += n
            for x in (2 * k, 2 * k + 1):
                for b in range(2):
                    m = m3[x0 + x + 2, b, y0 : y0 + n, :]
                    e0 = e0b[x0 + x + HALO, b, 8 + y0 : 8 + y0 + n, :]
                    put(eb, cb, HALO, x0 + x, b, e0 + m * part, y0)

    def correct_inner():
        def body(i, carry):
            correct_block(1 + 7 * i, 7, INNER)
            return carry

        lax.fori_loop(0, 2, body, 0)

    def correct_outer():
        for x in range(-2, NXL + 2):
            insert(e0b, se0.at[:, 0], HALO, x)
        correct_block(-1, 2, HALVES)
        correct_block(NXL // 2 - 1, 2, HALVES)
        correct_block(1, 14, OUTER)

    def smooth_rows(x0, count, half0):
        for x in range(count):
            insert(eb, se.at[:, 0], HALO, x0 + x)
        rem = stencil_rows(
            eb, HALO, x0, count, HALVES,
            lambda x, y0, n: h1s[half0 + x // 2 + 1, y0 : y0 + n, :],
        )
        d = split_mm(jnp.concatenate(list(rem.values()), axis=0), w0[...])
        return [(key, d[n * 32 : n * 32 + 32]) for n, key in enumerate(rem)]

    def smooth_edges():
        for x0, half0 in ((-1, -1), (NXL, NXL // 2)):
            for (x, y0, b), d in smooth_rows(x0, 1, half0):
                put(db, None, 1, x0 + x, b, d, y0)

    def smooth_part(j, i, acc):
        x0 = i * ROWS
        for (x, y0, b), d in smooth_rows(x0, ROWS, i * (ROWS // 2)):
            y = eb[x0 + x + HALO, b, 8 + y0 : 40 + y0, :] + d
            put(db, None, 1, x0 + x, b, d, y0)
            ys[j][x0 + x, b, y0 : y0 + 32, :] = y
            acc = acc + tile_sum(rhos[j][x0 + x + HALO, b, y0 : y0 + 32, :] * y)
        return acc

    def next_part(j, x0, count, acc):
        shift = HALO if j + 1 < ITERS else 0
        for x in range(count):
            insert(db, sd, 1, x0 + x)
        new = stencil_rows(db, 1, x0, count)
        for (x, y0, b), v in new.items():
            rhos[j + 1][x0 + x + shift, b, y0 : y0 + 32, :] = v
            acc = acc + tile_sum(v * ys[j][x0 + x, b, y0 : y0 + 32, :])
            if j + 1 < ITERS:
                put_sides(ss.at[j + 1], x0 + x, b, v, y0)
        return acc

    def smooth_and_next(j):
        zero = jnp.zeros((8, 128), F32)
        last = NXL // ROWS - 1
        smooth_edges()
        acc = lax.fori_loop(0, 2, lambda i, a: smooth_part(j, i * last, a), zero)
        acc_next = lax.fori_loop(0, 2, lambda i, a: next_part(j, i * (NXL - EDGE), EDGE, a), zero)
        if j + 1 < ITERS:
            send(j + 1, along_x)
        acc = lax.fori_loop(1, last, lambda i, a: smooth_part(j, i, a), acc)
        nus[2 * j] = acc
        acc_next = lax.fori_loop(
            0, 3, lambda i, a: next_part(j, EDGE + i * ROWS, ROWS, a), acc_next
        )
        if j + 1 < ITERS:
            send(j + 1, corners + along_y)
        nus[2 * j + 1] = acc_next

    dot_rows = lax.broadcasted_iota(jnp.int32, (8, 128), 0)
    here = pl.ds(32, NXL)

    def dot_row(n, v):
        return jnp.where(dot_rows == n, jnp.sum(v, axis=0, keepdims=True), 0.0)

    def mean_results():
        bar = [local(bars[n, here]) for n in range(ITERS + 1)]
        ybar = [local(ybars[n, here]) for n in range(ITERS)]
        part = dot_row(0, nu0)
        for n in range(2 * ITERS):
            v = 128.0 * tile_sum(bar[(n + 1) // 2] * ybar[n // 2])
            part = part + dot_row(n, v + nus[n] if n < 4 else v)
        dots[...] = part
        for n, v in enumerate(ybar + bar[1:]):
            to_columns(v)
            for b in range(2):
                cols[n, b] = tmat[pl.ds(b, NY2, stride=2), :]

    for j in range(ITERS):
        if j > 0:
            line_pass(j)
        correct_inner()
        if j == 1:
            mean_step(0)
            mean_step(1)
        if j == 2:
            mean_step(2)
            mean_results()
        receive(j)
        halo_lines(j)
        strip_correct()
        correct_outer()
        strip_smooth()
        smooth_and_next(j)

    part = dots[...]
    for n in (4, 5):
        part = part + dot_row(n, nus[n])
    total, copies = part, []
    for n, devs in enumerate(phases):
        red, base = reds[n], len(copies)
        red[0] = total
        for i, dev in enumerate(devs):
            copy = pltpu.make_async_remote_copy(
                src_ref=red.at[0], dst_ref=red.at[i + 1], send_sem=ss_sem.at[base + i],
                recv_sem=rs_sem.at[base + i], device_id=dev, device_id_type=MESH,
            )
            copy.start()
            copies.append(copy)
        for copy in copies[base:]:
            copy.wait_recv()
        total = jnp.sum(red[...], axis=0)
    total = jnp.broadcast_to(jnp.sum(total, axis=1, keepdims=True), (8, 128))
    nu = [total[n : n + 1] for n in range(2 * ITERS)]

    h00, h10, h20 = nu[0] - nu[1], nu[1] - nu[2], nu[2] - nu[3]
    h11, h21, h22 = nu[2] - nu[3], nu[3] - nu[4], nu[4] - nu[5]
    l10, l20 = h10 / h00, h20 / h00
    d1, s21 = h11 - l10 * h10, h21 - l10 * h20
    l21 = s21 / d1
    d2 = h22 - l20 * h20 - l21 * s21
    b1 = nu[1] - l10 * nu[0]
    b2 = nu[2] - l20 * nu[0] - l21 * b1
    c2 = b2 / d2
    c1 = b1 / d1 - l21 * c2
    c0 = nu[0] / h00 - l10 * c1 - l20 * c2
    a0, a1, a2 = 1.0 - c0, c0 - c1, c1 - c2

    xcols = [c0 * cols[0, b] + c1 * cols[1, b] + c2 * cols[2, b] for b in range(2)]
    rcols = [a1 * cols[3, b] + a2 * cols[4, b] + c2 * cols[5, b] for b in range(2)]

    for g in range(4):
        for x in range(8 * g, 8 * g + 8):
            for b in range(2):
                v = inp[x, pl.ds(b, NY2, stride=2), :]
                m = m3[x + 2, b]
                ox = c0 * y0[x, b] + c1 * y1[x, b] + c2 * y2[x, b]
                ox = ox + c0 * ((1.0 - m) * v) + xcols[b][:, x : x + 1]
                orr = a0 * v + a1 * rho1[x + HALO, b] + a2 * rho2[x + HALO, b] + c2 * rho3[x, b]
                orr = orr + rcols[b][:, x : x + 1]
                x_ref[x, pl.ds(b, NY2, stride=2), :] = ox
                r_ref[x, pl.ds(b, NY2, stride=2), :] = orr

    for i in range(8):
        pl.when(exists(*SIDES[i]))(lambda i=i: block_copy(i).wait_send())
        for j in range(ITERS):
            pl.when(exists(*SIDES[i]))(lambda i=i, j=j: face(j, i).wait_send())
    for copy in copies:
        copy.wait_send()


def shards(nx, ny, right_side, sea_mask, vertical_coupling):
    vmem = pltpu.VMEM
    sizes = {"x": nx // 8, "y": 4, "c": 2, "z": ny}
    counts = [math.prod(sizes[axis] for axis in axes) for axes in PHASES]
    counts = counts + [1] * (3 - len(counts))
    out = pltpu.VMEM(right_side.shape, F32)
    return pl.pallas_call(
        functools.partial(kernel, nx, ny),
        out_shape=(out, out),
        in_specs=[
            pl.BlockSpec(memory_space=pltpu.HBM),
            pl.BlockSpec(memory_space=pltpu.HBM),
            pl.BlockSpec(memory_space=pltpu.HBM),
        ],
        out_specs=(pl.BlockSpec(memory_space=vmem), pl.BlockSpec(memory_space=vmem)),
        scratch_shapes=[
            vmem((NXL, 128), jnp.int32),
            vmem((1, 127), F32),
            vmem((NXL, 128, 128), F32),
            vmem((NXL + 2 * HALO, 2, NY2, 128), F32),
            vmem((NXL + 2 * HALO, 2, NY2, 128), F32),
            vmem((NXL + 2 * HALO, 2, NY2, 128), F32),
            vmem((NXL, 2, NY2, 128), F32),
            vmem((NXL, 2, NY2, 128), F32),
            vmem((NXL, 2, NY2, 128), F32),
            vmem((NXL, 2, NY2, 128), F32),
            vmem((NXL + 2 * HALO, 2, 80, 128), F32),
            vmem((NXL + 2 * HALO, 2, 80, 128), F32),
            vmem((NXL + 2, 2, 80, 128), F32),
            vmem((NXL // 2 + 2, NY2, 128), F32),
            vmem((NXL + 4, 2, NY2, 128), F32),
            vmem((NXL + 4, 2, NY2, 128), F32),
            vmem((ITERS, 2, 3, 48, 128), F32),
            vmem((ITERS, 2, 3, NXL, 128), F32),
            vmem((2, 3, 48, 128), F32),
            vmem((2, 2, 48, 128), F32),
            vmem((2, 48, 128), F32),
            vmem((2, 48, 128), F32),
            vmem((2, 48, 128), F32),
            vmem((2, 2, 48, 128), F32),
            vmem((2, 2, 48, 128), F32),
            vmem((256, 256), BF16),
            vmem((256, 256), BF16),
            vmem((1, 128), F32),
            vmem((2 * NXL, 128), F32),
            vmem((8, 2 * NXL, 128), F32),
            vmem((128, 128), F32),
            vmem((4, 96, 256), F32),
            vmem((96, 256), F32),
            vmem((ITERS + 1, 96, 256), F32),
            vmem((ITERS, 96, 256), F32),
            vmem((2 * ITERS, 8, 128), F32),
            vmem((8, 128), F32),
            vmem((2 * ITERS, 2, NY2, 128), F32),
            *[vmem((n, 8, 128), F32) for n in counts],
            pltpu.SemaphoreType.DMA((3,)),
            pltpu.SemaphoreType.DMA((ITERS, 8)),
            pltpu.SemaphoreType.DMA((ITERS, 8)),
            pltpu.SemaphoreType.DMA((8,)),
            pltpu.SemaphoreType.DMA((8,)),
            pltpu.SemaphoreType.DMA((sum(counts),)),
            pltpu.SemaphoreType.DMA((sum(counts),)),
        ],
        compiler_params=pltpu.CompilerParams(
            collective_id=0, has_side_effects=True, vmem_limit_bytes=56 * 1024 * 1024
        ),
    )(right_side, sea_mask, vertical_coupling.reshape(1, -1))


def solution(mesh):
    nx, ny = mesh.shape["gx"], mesh.shape["gy"]
    return jax.shard_map(
        functools.partial(shards, nx, ny),
        mesh=mesh,
        in_specs=(P("gx", "gy", None), P("gx", "gy"), P()),
        out_specs=(P("gx", "gy", None), P("gx", "gy", None)),
        check_vma=False,
    )
```

```python
import functools
import itertools
import math

import jax
import jax.numpy as jnp
from jax import lax
from jax.experimental import pallas as pl
from jax.experimental.pallas import tpu as pltpu
from jax.sharding import PartitionSpec as P


ITERS = 3
SWEEPS = 4
F32 = jnp.float32
BF16 = jnp.bfloat16
MESH = pl.DeviceIdType.MESH
NXL, NY2, NZ = 32, 64, 128
ROWS = 8
HALO = 3
EDGE = 4
HALVES = ((0, 32), (32, 32))
INNER = ((8, 24), (32, 24))
OUTER = ((0, 8), (56, 8))
PHASES = ("cz", "xy")
SIDES = [(dx, dy) for dx in (-1, 0, 1) for dy in (-1, 0, 1) if (dx, dy) != (0, 0)]


def split_mm(v, w):
    high = v.astype(BF16)
    low = (v - high.astype(F32)).astype(BF16)
    o = jnp.dot(jnp.concatenate([high, low], axis=1), w, preferred_element_type=F32)
    return o[:, :128] + o[:, 128:]


def roll(v, shift, axis):
    return pltpu.roll(v, shift % v.shape[axis], axis)


def line_inverses(coupling, w_refs):
    lane = lax.broadcasted_iota(jnp.int32, (8, 128), 1)
    row = lax.broadcasted_iota(jnp.int32, (8, 128), 0)
    up = jnp.broadcast_to(coupling, (8, 128))
    lo = roll(up, 1, 1)
    factor = jnp.where(row == 0, 1.0, 4.0)
    diag = jnp.where(row == 0, 4.1, 4.4) + factor * (up + lo)
    off_up = factor * up
    off_lo = factor * lo

    def pivots(off, step):
        a, b = diag, -off * off
        c, d = jnp.ones_like(a), jnp.zeros_like(a)
        s = 1
        while s < 128:
            inside = (lane >= s) if step > 0 else (lane < 128 - s)
            ra = jnp.where(inside, roll(a, step * s, 1), 1.0)
            rb = jnp.where(inside, roll(b, step * s, 1), 0.0)
            rc = jnp.where(inside, roll(c, step * s, 1), 0.0)
            rd = jnp.where(inside, roll(d, step * s, 1), 1.0)
            na, nb = a * ra + b * rc, a * rb + b * rd
            nc, nd = c * ra + d * rc, c * rb + d * rd
            inv = 1.0 / na
            a, b, c, d = jnp.ones_like(a), nb * inv, nc * inv, nd * inv
            s *= 2
        return 1.0 / c

    fore = pivots(off_lo, 1)
    back = pivots(off_up, -1)
    main = 1.0 / (fore + back - diag)
    ratio = jnp.where(lane < 127, jnp.log(jnp.maximum(off_up, 1e-30) / fore), 0.0)
    total = jnp.where(lane >= 1, roll(ratio, 1, 1), 0.0)
    s = 1
    while s < 128:
        total = total + jnp.where(lane >= s, roll(total, s, 1), 0.0)
        s *= 2

    r = lax.broadcasted_iota(jnp.int32, (128, 128), 0)
    c = lax.broadcasted_iota(jnp.int32, (128, 128), 1)
    for i, w_ref in enumerate(w_refs):
        def wide(v):
            return jnp.broadcast_to(v[i : i + 1], (128, 128))

        g_row, t_row = wide(main), wide(total)
        g_col, t_col = g_row.T, t_row.T
        g = jnp.where(r <= c, g_row, g_col) * jnp.exp(-jnp.abs(t_row - t_col))
        a_col, u_col = wide(diag).T, wide(off_up).T
        l_col = wide(off_lo).T
        tg = a_col * g - u_col * roll(g, -1, 0) - l_col * roll(g, 1, 0)
        rest = jnp.where(r == c, 1.0, 0.0) - tg
        g = g + jnp.dot(g.astype(BF16), rest.astype(BF16), preferred_element_type=F32)
        high = g.astype(BF16)
        low = (g - high.astype(F32)).astype(BF16)
        both = jnp.concatenate([high, low], axis=1)
        w_ref[...] = jnp.concatenate([both, both], axis=0)


def kernel(
    nx, ny, rhs_ref, mask_hbm, coup_hbm, x_ref, r_ref,
    mask_ref, coup_ref, inp, rho0, rho1, rho2, rho3, y0, y1, y2, e0b, eb, db, h1s, m3, q3,
    sr, ss, se0, se, sd, cb0, cb, sm, sq, w0, w1, kpad,
    blk, nbr, tmat, mn, m2, bars, ybars, nus, dots, cols, red0, red1, red2,
    in_sem, sx_sem, rx_sem, sb_sem, rb_sem, ss_sem, rs_sem,
):
    gx, gy = lax.axis_index("gx"), lax.axis_index("gy")
    reds = (red0, red1, red2)
    rhos, ys = (rho0, rho1, rho2, rho3), (y0, y1, y2)

    sizes = {"x": nx // 8, "y": 4, "c": 2, "z": ny}
    place = {"x": lax.div(gx, 8), "y": lax.rem(lax.div(gx, 2), 4), "c": lax.rem(gx, 2), "z": gy}

    def partners(axes):
        devs = []
        for steps in itertools.product(*(range(sizes[axis]) for axis in axes)):
            if any(steps):
                at = dict(place)
                for axis, step in zip(axes, steps):
                    at[axis] = lax.rem(place[axis] + step, sizes[axis])
                devs.append((at["x"] * 8 + at["y"] * 2 + at["c"], at["z"]))
        return devs

    phases = [partners(axes) for axes in PHASES]

    def side_dev(dx, dy):
        return (lax.rem(gx + dx + nx, nx), lax.rem(gy + dy + ny, ny))

    small = [
        pltpu.make_async_copy(coup_hbm, coup_ref, in_sem.at[0]),
        pltpu.make_async_copy(mask_hbm, mask_ref, in_sem.at[1]),
    ]
    load = pltpu.make_async_copy(rhs_ref, inp, in_sem.at[2])
    for copy in small:
        copy.start()
    load.start()

    def clear(x, carry):
        zero = jnp.zeros((2, NY2, 128), F32)
        for rho in (rho0, rho1, rho2):
            rho[x] = zero
            rho[x + NXL + HALO] = zero
        return carry

    lax.fori_loop(0, HALO, clear, 0)
    sr[...] = jnp.zeros(sr.shape, F32)
    nbr[...] = jnp.zeros(nbr.shape, F32)
    cb0[...] = jnp.zeros(cb0.shape, F32)
    cb[...] = jnp.zeros(cb.shape, F32)

    barrier = pltpu.get_barrier_semaphore()
    for dx, dy in SIDES:
        pl.semaphore_signal(barrier, inc=1, device_id=side_dev(dx, dy), device_id_type=MESH)
    for dev in sum(phases, []):
        pl.semaphore_signal(barrier, inc=1, device_id=dev, device_id_type=MESH)

    for copy in small:
        copy.wait()
    kpad[...] = jnp.zeros((1, 128), F32)
    kpad[:, 0:127] = coup_ref[...]

    lane = lax.broadcasted_iota(jnp.int32, (NY2, 128), 1)

    def to_columns(v):
        tmat[...] = jnp.concatenate([v, jnp.zeros((128 - v.shape[0], 128), F32)], axis=0).T

    def expand(dst, start, stop, shift):
        for b in range(2):
            col = tmat[pl.ds(b, NY2, stride=2), :]
            for x in range(start, stop):
                dst[x + shift, b] = jnp.broadcast_to(col[:, x : x + 1], (NY2, 128))

    mask = mask_ref[...].astype(F32)
    blk[0:NXL, :] = mask
    to_columns(mask)
    expand(m3, 0, NXL, 2)

    def put_sides(dst, x, b, v, y0=0):
        n = v.shape[0]
        for half, d, row in (
            ((0, 0, 0), (0, 2, 1), (1, 1, n - 1)) if b == 0 else ((0, 1, 0), (1, 0, n - 1), (1, 2, n - 2))
        ):
            if y0 == 0 if half == 0 else y0 + n == NY2:
                dst[half, d, pl.ds(x, 1), :] = v[row : row + 1]

    def put(dst, edge, shift, x, b, v, y0=0):
        n = v.shape[0]
        dst[x + shift, b, 8 + y0 : 8 + y0 + n, :] = v
        if edge is not None and (y0 == 0 if b == 0 else y0 + n == NY2):
            edge[b, pl.ds(x + 8, 1), :] = v[0:1] if b == 0 else v[n - 1 : n]

    def tile_sum(v):
        return jnp.sum(v.reshape(-1, 8, 128), axis=0)

    load.wait()

    def start_pass(i, carry):
        acc, means = carry[0], list(carry[1:])
        for x, b in [(i * 4 + k, b) for k in range(4) for b in range(2)]:
            v = inp[x, pl.ds(b, NY2, stride=2), :]
            m = m3[x + 2, b]
            mean = jnp.sum(v, axis=1, keepdims=True) * (1.0 / NZ)
            means[b] = jnp.where(lane == x, mean, means[b])
            dev = m * (v - mean)
            rho0[x + HALO, b] = dev
            put_sides(ss.at[0], x, b, dev)
            land = (1.0 - m) * v
            acc = acc + tile_sum(land * land)
        return (acc, *means)

    zero = jnp.zeros((NY2, 128), F32)
    nu0, mean0, mean1 = lax.fori_loop(0, NXL // 4, start_pass, (jnp.zeros((8, 128), F32), zero, zero))
    tmat[pl.ds(0, NY2, stride=2), :] = mean0
    tmat[pl.ds(1, NY2, stride=2), :] = mean1
    blk[NXL : 2 * NXL, :] = mask * tmat[...].T[0:NXL]

    pl.semaphore_wait(barrier, len(SIDES) + sum(map(len, phases)))

    def exists(dx, dy):
        ok = None
        for pos, d, n in ((gx, dx, nx), (gy, dy, ny)):
            if d:
                here = (pos + d >= 0) & (pos + d < n)
                ok = here if ok is None else ok & here
        return ok

    def block_copy(i):
        return pltpu.make_async_remote_copy(
            src_ref=blk, dst_ref=nbr.at[i], send_sem=sb_sem.at[i], recv_sem=rb_sem.at[i],
            device_id=side_dev(*SIDES[i]), device_id_type=MESH,
        )

    def face(j, i):
        dx, dy = SIDES[i]
        if dy == 0:
            src = rhos[j].at[pl.ds(HALO if dx < 0 else NXL, HALO)]
            dst = rhos[j].at[pl.ds(NXL + HALO if dx < 0 else 0, HALO)]
        else:
            s = 0 if dy < 0 else 1
            x0, n, to = {-1: (0, 8, 40), 0: (0, NXL, 8), 1: (NXL - 8, 8, 0)}[dx]
            src = ss.at[j, s, :, pl.ds(x0, n), :]
            dst = sr.at[j, 1 - s, :, pl.ds(to, n), :]
        return pltpu.make_async_remote_copy(
            src_ref=src, dst_ref=dst, send_sem=sx_sem.at[j, i], recv_sem=rx_sem.at[j, i],
            device_id=side_dev(dx, dy), device_id_type=MESH,
        )

    along_x = [i for i, (dx, dy) in enumerate(SIDES) if dy == 0]
    along_y = [i for i, (dx, dy) in enumerate(SIDES) if dx == 0]
    corners = [i for i, (dx, dy) in enumerate(SIDES) if dx and dy]

    def send(j, which):
        for i in which:
            pl.when(exists(*SIDES[i]))(lambda i=i: face(j, i).start())

    def sent(j):
        for i in range(8):
            pl.when(exists(*SIDES[i]))(lambda i=i: face(j, i).wait_send())
            if j == 0:
                pl.when(exists(*SIDES[i]))(lambda i=i: block_copy(i).wait_send())

    def receive(j):
        for i, (dx, dy) in enumerate(SIDES):
            pl.when(exists(-dx, -dy))(lambda i=i: face(j, i).wait_recv())

    for i in corners + along_x + along_y:
        pl.when(exists(*SIDES[i]))(lambda i=i: block_copy(i).start())
    send(0, along_x + corners + along_y)
    line_inverses(kpad[...], (w0, w1))

    def line_pass(j):
        def body(i, carry):
            for x8 in range(ROWS):
                x = i * ROWS + x8
                e0 = split_mm(rhos[j][x + HALO].reshape(128, 128), w0[...])
                put(e0b, cb0, HALO, x, 0, e0[:NY2])
                put(e0b, cb0, HALO, x, 1, e0[NY2:])
            return carry

        lax.fori_loop(0, NXL // ROWS, body, 0)

    line_pass(0)

    for i in range(8):
        dx, dy = SIDES[i]
        pl.when(exists(-dx, -dy))(lambda i=i: block_copy(i).wait_recv())

    low_half = lax.broadcasted_iota(jnp.int32, (96, 128), 1) < 64

    def around(rows):
        def column(dy):
            parts = []
            for dx in (-1, 0, 1):
                if (dx, dy) == (0, 0):
                    parts.append(blk[rows, :])
                else:
                    parts.append(nbr[SIDES.index((-dx, -dy)), rows, :])
            return roll(jnp.concatenate(parts, axis=0), 64, 1)

        left, mid, right = column(-1), column(0), column(1)
        return jnp.concatenate(
            [jnp.where(low_half, left, mid), jnp.where(low_half, mid, right)], axis=1
        )

    def local(v):
        a, b = roll(v[:, 0:128], 64, 1), roll(v[:, 128:256], 64, 1)
        return jnp.where(low_half[: v.shape[0]], a, b)

    moves = ((-1, 0), (1, 0), (-1, 1), (1, 1))
    mask2 = around(pl.ds(0, NXL))
    m2[...] = mask2
    bars[0] = around(pl.ds(NXL, NXL))
    open_sides = jnp.zeros((96, 256), F32)
    for i, (s, axis) in enumerate(moves):
        beside = roll(mask2, s, axis)
        mn[i] = beside
        open_sides = open_sides + beside
    own2 = mask2 * (4.0 - open_sides)
    to_columns(local(mask2[24:72]))
    expand(m3, 6, 8, -6)
    expand(m3, 40, 42, -6)
    to_columns(local(own2[24:72]))
    expand(q3, 6, 42, -6)
    for a in range(2):
        for s, at in ((0, 63 - a), (1, 192 + a)):
            sm[s, a] = jnp.broadcast_to(mask2[24:72, at : at + 1], (48, 128))
            sq[s, a] = jnp.broadcast_to(own2[24:72, at : at + 1], (48, 128))

    xi = lax.broadcasted_iota(jnp.int32, (96, 256), 0) + (gx * NXL - 32)
    yi = lax.broadcasted_iota(jnp.int32, (96, 256), 1) + (gy * 128 - 64)
    inside = (xi >= 0) & (xi < nx * NXL) & (yi >= 0) & (yi < ny * 128)
    dom = jnp.where(inside, 1.0, 0.0)

    even_x = lax.rem(lax.broadcasted_iota(jnp.int32, (96, 256), 0), 2) == 0
    even_y = lax.rem(lax.broadcasted_iota(jnp.int32, (96, 256), 1), 2) == 0
    even_s = lax.rem(lax.broadcasted_iota(jnp.int32, (48, 128), 0), 2) == 0

    def flow(v):
        total = None
        for i, (s, axis) in enumerate(moves):
            term = mn[i] * (roll(v, s, axis) - v)
            total = term if total is None else total + term
        return total

    def mean_step(j):
        m = m2[...]
        e0 = bars[j] * (1.0 / 4.1)
        t = 4.0 * e0 + flow(e0)
        t1 = m * t
        t1 = t1 + jnp.where(even_x, roll(t1, -1, 0), roll(t1, 1, 0))
        t1 = t1 + jnp.where(even_y, roll(t1, -1, 1), roll(t1, 1, 1))
        e1 = t1 * (1.0 / 4.4)
        c = (0.8 / 4.4) * t1
        for _ in range(SWEEPS - 1):
            beside = (roll(c, 2, 0) + roll(c, -2, 0)) + (roll(c, 2, 1) + roll(c, -2, 1))
            c = dom * (c + 0.8 * (t1 - (4.4 * c - beside)) / 4.4)
        f = e1 + c
        rem = m * (t + flow(f) + (e1 - 0.25 * t1) - 0.1 * c)
        d = rem * (1.0 / 4.1)
        ybars[j] = e0 + m * f + d
        bars[j + 1] = m * (4.0 * d + flow(d))

    def insert(dst, src, shift, x):
        dst[x + shift, 1, 7:8, :] = src[0, pl.ds(x + 8, 1), :]
        dst[x + shift, 0, 72:73, :] = src[1, pl.ds(x + 8, 1), :]

    def stencil_rows(src, shift, x0, count, parts=HALVES, less=None):
        out = {}
        for y0, n in parts:
            held = {}

            def centre(x, b):
                if (x, b) not in held:
                    held[x, b] = src[x0 + x + shift, b, 8 + y0 : 8 + y0 + n, :]
                return held[x, b]

            for x in range(count):
                minus = None if less is None else less(x, y0, n)
                for b in range(2):
                    at = 7 + y0 if b == 0 else 9 + y0
                    beside = centre(x, 1 - b) + src[x0 + x + shift, 1 - b, at : at + n, :]
                    beside = beside + (centre(x - 1, b) + centre(x + 1, b))
                    if minus is not None:
                        beside = beside - minus
                    q = q3[x0 + x + 2, b, y0 : y0 + n, :]
                    m = m3[x0 + x + 2, b, y0 : y0 + n, :]
                    out[x, y0, b] = q * centre(x, b) + m * beside
        return out

    def strip_beside(v):
        return roll(v, 1, 0) + roll(v, -1, 0)

    def halo_lines(j):
        for x in (-3, -2, -1, 32, 33, 34):
            e0 = split_mm(rhos[j][x + HALO].reshape(128, 128), w0[...])
            put(e0b, cb0, HALO, x, 0, e0[:NY2])
            put(e0b, cb0, HALO, x, 1, e0[NY2:])
        se0[...] = split_mm(sr[j].reshape(288, 128), w0[...]).reshape(2, 3, 48, 128)

    def strip_correct():
        t1 = []
        for s in range(2):
            near, mid, far = se0[s, 0], se0[s, 1], se0[s, 2]
            t = sq[s, 0] * near + sm[s, 0] * (cb0[s] + mid + strip_beside(near))
            t = t + sq[s, 1] * mid + sm[s, 1] * (near + far + strip_beside(mid))
            t1.append(t + jnp.where(even_s, roll(t, -1, 0), roll(t, 1, 0)))
        t1 = jnp.concatenate(t1, axis=0)
        e1 = split_mm(t1, w1[...])
        h1 = 0.25 * t1 + 3.0 * e1
        for s in range(2):
            part = e1[48 * s : 48 * s + 48]
            for a in range(2):
                se[s, a] = se0[s, a] + sm[s, a] * part
            sd[s] = h1[48 * s : 48 * s + 48]

    def strip_smooth():
        rem = []
        for s in range(2):
            near, far = se[s, 0], se[s, 1]
            rem.append(sq[s, 0] * near + sm[s, 0] * (cb[s] + far + strip_beside(near) - sd[s]))
        sd[...] = split_mm(jnp.concatenate(rem, axis=0), w0[...]).reshape(2, 48, 128)

    def correct_block(first, count, parts):
        x0 = 2 * first
        t = stencil_rows(e0b, HALO, x0, 2 * count, parts)
        keys = [(k, y0, n) for y0, n in parts for k in range(count)]
        t1 = jnp.concatenate(
            [
                (t[2 * k, y0, 0] + t[2 * k, y0, 1]) + (t[2 * k + 1, y0, 0] + t[2 * k + 1, y0, 1])
                for k, y0, n in keys
            ],
            axis=0,
        )
        e1 = split_mm(t1, w1[...])
        h1 = 0.25 * t1 + 3.0 * e1
        at = 0
        for k, y0, n in keys:
            part = e1[at : at + n]
            h1s[first + k + 1, y0 : y0 + n, :] = h1[at : at + n]
            at += n
            for x in (2 * k, 2 * k + 1):
                for b in range(2):
                    m = m3[x0 + x + 2, b, y0 : y0 + n, :]
                    e0 = e0b[x0 + x + HALO, b, 8 + y0 : 8 + y0 + n, :]
                    put(eb, cb, HALO, x0 + x, b, e0 + m * part, y0)

    def correct_inner():
        def body(i, carry):
            correct_block(1 + 7 * i, 7, INNER)
            return carry

        lax.fori_loop(0, 2, body, 0)

    def correct_outer():
        for x in range(-2, NXL + 2):
            insert(e0b, se0.at[:, 0], HALO, x)
        correct_block(-1, 2, HALVES)
        correct_block(NXL // 2 - 1, 2, HALVES)
        correct_block(1, 14, OUTER)

    def smooth_rows(x0, count, half):
        for x in range(count):
            insert(eb, se.at[:, 0], HALO, x0 + x)
        rem = stencil_rows(
            eb, HALO, x0, count, HALVES,
            lambda x, y0, n: h1s[half(x) + 1, y0 : y0 + n, :],
        )
        d = split_mm(jnp.concatenate(list(rem.values()), axis=0), w0[...])
        return [(key, d[n * 32 : n * 32 + 32]) for n, key in enumerate(rem)]

    def smooth_put(j, x, y0, b, d, acc):
        y = eb[x + HALO, b, 8 + y0 : 40 + y0, :] + d
        put(db, None, 1, x, b, d, y0)
        ys[j][x, b, y0 : y0 + 32, :] = y
        return acc + tile_sum(rhos[j][x + HALO, b, y0 : y0 + 32, :] * y)

    def smooth_edges(j, acc):
        for x0 in (-1, NXL - EDGE):
            for (x, y0, b), d in smooth_rows(x0, EDGE + 1, lambda x: (x0 + x) // 2):
                if 0 <= x0 + x < NXL:
                    acc = smooth_put(j, x0 + x, y0, b, d, acc)
                else:
                    put(db, None, 1, x0 + x, b, d, y0)
        return acc

    def smooth_part(j, i, acc):
        x0 = EDGE + i * ROWS
        for (x, y0, b), d in smooth_rows(
            x0, ROWS, lambda x: EDGE // 2 + i * (ROWS // 2) + x // 2
        ):
            acc = smooth_put(j, x0 + x, y0, b, d, acc)
        return acc

    def next_part(j, x0, count, acc):
        shift = HALO if j + 1 < ITERS else 0
        for x in range(count):
            insert(db, sd, 1, x0 + x)
        new = stencil_rows(db, 1, x0, count)
        for (x, y0, b), v in new.items():
            rhos[j + 1][x0 + x + shift, b, y0 : y0 + 32, :] = v
            acc = acc + tile_sum(v * ys[j][x0 + x, b, y0 : y0 + 32, :])
            if j + 1 < ITERS:
                put_sides(ss.at[j + 1], x0 + x, b, v, y0)
        return acc

    def smooth_and_next(j):
        zero = jnp.zeros((8, 128), F32)
        acc = smooth_edges(j, zero)
        acc_next = next_part(j, 0, HALO, zero)
        acc_next = next_part(j, NXL - HALO, HALO, acc_next)
        if j + 1 < ITERS:
            send(j + 1, along_x)
        nus[2 * j] = lax.fori_loop(0, 3, lambda i, a: smooth_part(j, i, a), acc)
        inner = (NXL - 2 * HALO) // 2
        acc_next = lax.fori_loop(
            0, 2, lambda i, a: next_part(j, HALO + i * inner, inner, a), acc_next
        )
        if j + 1 < ITERS:
            send(j + 1, corners + along_y)
        nus[2 * j + 1] = acc_next

    dot_rows = lax.broadcasted_iota(jnp.int32, (8, 128), 0)
    here = pl.ds(32, NXL)

    def dot_row(n, v):
        return jnp.where(dot_rows == n, jnp.sum(v, axis=0, keepdims=True), 0.0)

    def mean_results():
        bar = [local(bars[n, here]) for n in range(ITERS + 1)]
        ybar = [local(ybars[n, here]) for n in range(ITERS)]
        part = dot_row(0, nu0)
        for n in range(2 * ITERS):
            v = 128.0 * tile_sum(bar[(n + 1) // 2] * ybar[n // 2])
            part = part + dot_row(n, v + nus[n] if n < 4 else v)
        dots[...] = part
        for n, v in enumerate(ybar + bar[1:]):
            to_columns(v)
            for b in range(2):
                cols[n, b] = tmat[pl.ds(b, NY2, stride=2), :]

    for j in range(ITERS):
        if j > 0:
            line_pass(j)
            sent(j - 1)
        correct_inner()
        if j == 1:
            mean_step(0)
            mean_step(1)
        if j == 2:
            mean_step(2)
            mean_results()
        receive(j)
        halo_lines(j)
        strip_correct()
        correct_outer()
        strip_smooth()
        smooth_and_next(j)

    part = dots[...]
    for n in (4, 5):
        part = part + dot_row(n, nus[n])
    total, copies = part, []
    for n, devs in enumerate(phases):
        red, base = reds[n], len(copies)
        red[0] = total
        for i, dev in enumerate(devs):
            copy = pltpu.make_async_remote_copy(
                src_ref=red.at[0], dst_ref=red.at[i + 1], send_sem=ss_sem.at[base + i],
                recv_sem=rs_sem.at[n], device_id=dev, device_id_type=MESH,
            )
            copy.start()
            copies.append(copy)
        if n == 1:
            sent(ITERS - 1)
            for copy in copies[:base]:
                copy.wait_send()
        rest = red.at[pl.ds(1, len(devs))]
        pltpu.make_async_copy(rest, rest, rs_sem.at[n]).wait()
        total = jnp.sum(red[...], axis=0)
    total = jnp.broadcast_to(jnp.sum(total, axis=1, keepdims=True), (8, 128))
    nu = [total[n : n + 1] for n in range(2 * ITERS)]

    h00, h10, h20 = nu[0] - nu[1], nu[1] - nu[2], nu[2] - nu[3]
    h11, h21, h22 = nu[2] - nu[3], nu[3] - nu[4], nu[4] - nu[5]
    l10, l20 = h10 / h00, h20 / h00
    d1, s21 = h11 - l10 * h10, h21 - l10 * h20
    l21 = s21 / d1
    d2 = h22 - l20 * h20 - l21 * s21
    b1 = nu[1] - l10 * nu[0]
    b2 = nu[2] - l20 * nu[0] - l21 * b1
    c2 = b2 / d2
    c1 = b1 / d1 - l21 * c2
    c0 = nu[0] / h00 - l10 * c1 - l20 * c2
    a0, a1, a2 = 1.0 - c0, c0 - c1, c1 - c2

    xcols = [c0 * cols[0, b] + c1 * cols[1, b] + c2 * cols[2, b] for b in range(2)]
    rcols = [a1 * cols[3, b] + a2 * cols[4, b] + c2 * cols[5, b] for b in range(2)]

    for g in range(4):
        for x in range(8 * g, 8 * g + 8):
            for b in range(2):
                v = inp[x, pl.ds(b, NY2, stride=2), :]
                m = m3[x + 2, b]
                ox = c0 * y0[x, b] + c1 * y1[x, b] + c2 * y2[x, b]
                ox = ox + c0 * ((1.0 - m) * v) + xcols[b][:, x : x + 1]
                orr = a0 * v + a1 * rho1[x + HALO, b] + a2 * rho2[x + HALO, b] + c2 * rho3[x, b]
                orr = orr + rcols[b][:, x : x + 1]
                x_ref[x, pl.ds(b, NY2, stride=2), :] = ox
                r_ref[x, pl.ds(b, NY2, stride=2), :] = orr

    for copy in copies[len(phases[0]):]:
        copy.wait_send()


def shards(nx, ny, right_side, sea_mask, vertical_coupling):
    vmem = pltpu.VMEM
    sizes = {"x": nx // 8, "y": 4, "c": 2, "z": ny}
    counts = [math.prod(sizes[axis] for axis in axes) for axes in PHASES]
    counts = counts + [1] * (3 - len(counts))
    out = pltpu.VMEM(right_side.shape, F32)
    return pl.pallas_call(
        functools.partial(kernel, nx, ny),
        out_shape=(out, out),
        in_specs=[
            pl.BlockSpec(memory_space=pltpu.HBM),
            pl.BlockSpec(memory_space=pltpu.HBM),
            pl.BlockSpec(memory_space=pltpu.HBM),
        ],
        out_specs=(pl.BlockSpec(memory_space=vmem), pl.BlockSpec(memory_space=vmem)),
        scratch_shapes=[
            vmem((NXL, 128), jnp.int32),
            vmem((1, 127), F32),
            vmem((NXL, 128, 128), F32),
            vmem((NXL + 2 * HALO, 2, NY2, 128), F32),
            vmem((NXL + 2 * HALO, 2, NY2, 128), F32),
            vmem((NXL + 2 * HALO, 2, NY2, 128), F32),
            vmem((NXL, 2, NY2, 128), F32),
            vmem((NXL, 2, NY2, 128), F32),
            vmem((NXL, 2, NY2, 128), F32),
            vmem((NXL, 2, NY2, 128), F32),
            vmem((NXL + 2 * HALO, 2, 80, 128), F32),
            vmem((NXL + 2 * HALO, 2, 80, 128), F32),
            vmem((NXL + 2, 2, 80, 128), F32),
            vmem((NXL // 2 + 2, NY2, 128), F32),
            vmem((NXL + 4, 2, NY2, 128), F32),
            vmem((NXL + 4, 2, NY2, 128), F32),
            vmem((ITERS, 2, 3, 48, 128), F32),
            vmem((ITERS, 2, 3, NXL, 128), F32),
            vmem((2, 3, 48, 128), F32),
            vmem((2, 2, 48, 128), F32),
            vmem((2, 48, 128), F32),
            vmem((2, 48, 128), F32),
            vmem((2, 48, 128), F32),
            vmem((2, 2, 48, 128), F32),
            vmem((2, 2, 48, 128), F32),
            vmem((256, 256), BF16),
            vmem((256, 256), BF16),
            vmem((1, 128), F32),
            vmem((2 * NXL, 128), F32),
            vmem((8, 2 * NXL, 128), F32),
            vmem((128, 128), F32),
            vmem((4, 96, 256), F32),
            vmem((96, 256), F32),
            vmem((ITERS + 1, 96, 256), F32),
            vmem((ITERS, 96, 256), F32),
            vmem((2 * ITERS, 8, 128), F32),
            vmem((8, 128), F32),
            vmem((2 * ITERS, 2, NY2, 128), F32),
            *[vmem((n, 8, 128), F32) for n in counts],
            pltpu.SemaphoreType.DMA((3,)),
            pltpu.SemaphoreType.DMA((ITERS, 8)),
            pltpu.SemaphoreType.DMA((ITERS, 8)),
            pltpu.SemaphoreType.DMA((8,)),
            pltpu.SemaphoreType.DMA((8,)),
            pltpu.SemaphoreType.DMA((sum(counts),)),
            pltpu.SemaphoreType.DMA((2,)),
        ],
        compiler_params=pltpu.CompilerParams(
            collective_id=0, has_side_effects=True, vmem_limit_bytes=56 * 1024 * 1024
        ),
    )(right_side, sea_mask, vertical_coupling.reshape(1, -1))


def solution(mesh):
    nx, ny = mesh.shape["gx"], mesh.shape["gy"]
    return jax.shard_map(
        functools.partial(shards, nx, ny),
        mesh=mesh,
        in_specs=(P("gx", "gy", None), P("gx", "gy"), P()),
        out_specs=(P("gx", "gy", None), P("gx", "gy", None)),
        check_vma=False,
    )
```

```python
import functools
import itertools
import math

import jax
import jax.numpy as jnp
from jax import lax
from jax.experimental import pallas as pl
from jax.experimental.pallas import tpu as pltpu
from jax.sharding import PartitionSpec as P


ITERS = 3
SWEEPS = 4
F32 = jnp.float32
BF16 = jnp.bfloat16
MESH = pl.DeviceIdType.MESH
NXL, NY2, NZ = 32, 64, 128
ROWS = 8
HALO = 3
EDGE = 4
MID = 12
HALVES = ((0, 32), (32, 32))
INNER = ((8, 24), (32, 24))
OUTER = ((0, 8), (56, 8))
PHASES = ("cz", "xy")
SIDES = [(dx, dy) for dx in (-1, 0, 1) for dy in (-1, 0, 1) if (dx, dy) != (0, 0)]


def split_mm(v, w):
    high = v.astype(BF16)
    low = (v - high.astype(F32)).astype(BF16)
    o = jnp.dot(jnp.concatenate([high, low], axis=1), w, preferred_element_type=F32)
    return o[:, :128] + o[:, 128:]


def roll(v, shift, axis):
    return pltpu.roll(v, shift % v.shape[axis], axis)


def line_inverses(coupling, w_refs):
    lane = lax.broadcasted_iota(jnp.int32, (8, 128), 1)
    row = lax.broadcasted_iota(jnp.int32, (8, 128), 0)
    up = jnp.broadcast_to(coupling, (8, 128))
    lo = roll(up, 1, 1)
    factor = jnp.where(row == 0, 1.0, 4.0)
    diag = jnp.where(row == 0, 4.1, 4.4) + factor * (up + lo)
    off_up = factor * up
    off_lo = factor * lo

    def pivots(off, step):
        a, b = diag, -off * off
        c, d = jnp.ones_like(a), jnp.zeros_like(a)
        s = 1
        while s < 128:
            inside = (lane >= s) if step > 0 else (lane < 128 - s)
            ra = jnp.where(inside, roll(a, step * s, 1), 1.0)
            rb = jnp.where(inside, roll(b, step * s, 1), 0.0)
            rc = jnp.where(inside, roll(c, step * s, 1), 0.0)
            rd = jnp.where(inside, roll(d, step * s, 1), 1.0)
            na, nb = a * ra + b * rc, a * rb + b * rd
            nc, nd = c * ra + d * rc, c * rb + d * rd
            inv = 1.0 / na
            a, b, c, d = jnp.ones_like(a), nb * inv, nc * inv, nd * inv
            s *= 2
        return 1.0 / c

    fore = pivots(off_lo, 1)
    back = pivots(off_up, -1)
    main = 1.0 / (fore + back - diag)
    ratio = jnp.where(lane < 127, jnp.log(jnp.maximum(off_up, 1e-30) / fore), 0.0)
    total = jnp.where(lane >= 1, roll(ratio, 1, 1), 0.0)
    s = 1
    while s < 128:
        total = total + jnp.where(lane >= s, roll(total, s, 1), 0.0)
        s *= 2

    r = lax.broadcasted_iota(jnp.int32, (128, 128), 0)
    c = lax.broadcasted_iota(jnp.int32, (128, 128), 1)
    for i, w_ref in enumerate(w_refs):
        def wide(v):
            return jnp.broadcast_to(v[i : i + 1], (128, 128))

        g_row, t_row = wide(main), wide(total)
        g_col, t_col = g_row.T, t_row.T
        g = jnp.where(r <= c, g_row, g_col) * jnp.exp(-jnp.abs(t_row - t_col))
        a_col, u_col = wide(diag).T, wide(off_up).T
        l_col = wide(off_lo).T
        tg = a_col * g - u_col * roll(g, -1, 0) - l_col * roll(g, 1, 0)
        rest = jnp.where(r == c, 1.0, 0.0) - tg
        g = g + jnp.dot(g.astype(BF16), rest.astype(BF16), preferred_element_type=F32)
        high = g.astype(BF16)
        low = (g - high.astype(F32)).astype(BF16)
        both = jnp.concatenate([high, low], axis=1)
        w_ref[...] = jnp.concatenate([both, both], axis=0)


def kernel(
    nx, ny, rhs_ref, mask_hbm, coup_hbm, x_ref, r_ref,
    mask_ref, coup_ref, inp, rho0, rho1, rho2, rho3, y0, y1, y2, e0b, eb, db, h1s, m3, q3,
    sr, ss, se0, se, sd, cb0, cb, sm, sq, w0, w1, kpad,
    blk, nbr, tmat, mn, m2, bars, ybars, nus, dots, cols, red0, red1, red2,
    in_sem, sx_sem, rx_sem, sb_sem, rb_sem, ss_sem, rs_sem,
):
    gx, gy = lax.axis_index("gx"), lax.axis_index("gy")
    reds = (red0, red1, red2)
    rhos, ys = (rho0, rho1, rho2, rho3), (y0, y1, y2)

    sizes = {"x": nx // 8, "y": 4, "c": 2, "z": ny}
    place = {"x": lax.div(gx, 8), "y": lax.rem(lax.div(gx, 2), 4), "c": lax.rem(gx, 2), "z": gy}

    def partners(axes):
        devs = []
        for steps in itertools.product(*(range(sizes[axis]) for axis in axes)):
            if any(steps):
                at = dict(place)
                for axis, step in zip(axes, steps):
                    at[axis] = lax.rem(place[axis] + step, sizes[axis])
                devs.append((at["x"] * 8 + at["y"] * 2 + at["c"], at["z"]))
        return devs

    phases = [partners(axes) for axes in PHASES]

    def side_dev(dx, dy):
        return (lax.rem(gx + dx + nx, nx), lax.rem(gy + dy + ny, ny))

    small = [
        pltpu.make_async_copy(coup_hbm, coup_ref, in_sem.at[0]),
        pltpu.make_async_copy(mask_hbm, mask_ref, in_sem.at[1]),
    ]
    load = pltpu.make_async_copy(rhs_ref, inp, in_sem.at[2])
    for copy in small:
        copy.start()
    load.start()

    def clear(x, carry):
        zero = jnp.zeros((2, NY2, 128), F32)
        for rho in (rho0, rho1, rho2):
            rho[x] = zero
            rho[x + NXL + HALO] = zero
        return carry

    lax.fori_loop(0, HALO, clear, 0)
    sr[...] = jnp.zeros(sr.shape, F32)
    nbr[...] = jnp.zeros(nbr.shape, F32)
    cb0[...] = jnp.zeros(cb0.shape, F32)
    cb[...] = jnp.zeros(cb.shape, F32)

    barrier = pltpu.get_barrier_semaphore()
    for dx, dy in SIDES:
        pl.semaphore_signal(barrier, inc=1, device_id=side_dev(dx, dy), device_id_type=MESH)
    for dev in sum(phases, []):
        pl.semaphore_signal(barrier, inc=1, device_id=dev, device_id_type=MESH)

    for copy in small:
        copy.wait()
    kpad[...] = jnp.zeros((1, 128), F32)
    kpad[:, 0:127] = coup_ref[...]

    lane = lax.broadcasted_iota(jnp.int32, (NY2, 128), 1)

    def to_columns(v):
        tmat[...] = jnp.concatenate([v, jnp.zeros((128 - v.shape[0], 128), F32)], axis=0).T

    def expand(dst, start, stop, shift):
        for b in range(2):
            col = tmat[pl.ds(b, NY2, stride=2), :]
            for x in range(start, stop):
                dst[x + shift, b] = jnp.broadcast_to(col[:, x : x + 1], (NY2, 128))

    mask = mask_ref[...].astype(F32)
    blk[0:NXL, :] = mask
    to_columns(mask)
    expand(m3, 0, NXL, 2)

    def put_sides(dst, x, b, v, y0=0):
        n = v.shape[0]
        for half, d, row in (
            ((0, 0, 0), (0, 2, 1), (1, 1, n - 1)) if b == 0 else ((0, 1, 0), (1, 0, n - 1), (1, 2, n - 2))
        ):
            if y0 == 0 if half == 0 else y0 + n == NY2:
                dst[half, d, pl.ds(x, 1), :] = v[row : row + 1]

    def put(dst, edge, shift, x, b, v, y0=0):
        n = v.shape[0]
        dst[x + shift, b, 8 + y0 : 8 + y0 + n, :] = v
        if edge is not None and (y0 == 0 if b == 0 else y0 + n == NY2):
            edge[b, pl.ds(x + 8, 1), :] = v[0:1] if b == 0 else v[n - 1 : n]

    def tile_sum(v):
        return jnp.sum(v.reshape(-1, 8, 128), axis=0)

    load.wait()

    def start_pass(i, carry):
        acc, means = carry[0], list(carry[1:])
        for x, b in [(i * 4 + k, b) for k in range(4) for b in range(2)]:
            v = inp[x, pl.ds(b, NY2, stride=2), :]
            m = m3[x + 2, b]
            mean = jnp.sum(v, axis=1, keepdims=True) * (1.0 / NZ)
            means[b] = jnp.where(lane == x, mean, means[b])
            dev = m * (v - mean)
            rho0[x + HALO, b] = dev
            put_sides(ss.at[0], x, b, dev)
            land = (1.0 - m) * v
            acc = acc + tile_sum(land * land)
        return (acc, *means)

    zero = jnp.zeros((NY2, 128), F32)
    nu0, mean0, mean1 = lax.fori_loop(0, NXL // 4, start_pass, (jnp.zeros((8, 128), F32), zero, zero))
    tmat[pl.ds(0, NY2, stride=2), :] = mean0
    tmat[pl.ds(1, NY2, stride=2), :] = mean1
    blk[NXL : 2 * NXL, :] = mask * tmat[...].T[0:NXL]

    pl.semaphore_wait(barrier, len(SIDES) + sum(map(len, phases)))

    def exists(dx, dy):
        ok = None
        for pos, d, n in ((gx, dx, nx), (gy, dy, ny)):
            if d:
                here = (pos + d >= 0) & (pos + d < n)
                ok = here if ok is None else ok & here
        return ok

    def block_copy(i):
        return pltpu.make_async_remote_copy(
            src_ref=blk, dst_ref=nbr.at[i], send_sem=sb_sem.at[i], recv_sem=rb_sem.at[i],
            device_id=side_dev(*SIDES[i]), device_id_type=MESH,
        )

    def face(j, i):
        dx, dy = SIDES[i]
        if dy == 0:
            src = rhos[j].at[pl.ds(HALO if dx < 0 else NXL, HALO)]
            dst = rhos[j].at[pl.ds(NXL + HALO if dx < 0 else 0, HALO)]
        else:
            s = 0 if dy < 0 else 1
            x0, n, to = {-1: (0, 8, 40), 0: (0, NXL, 8), 1: (NXL - 8, 8, 0)}[dx]
            src = ss.at[j, s, :, pl.ds(x0, n), :]
            dst = sr.at[j, 1 - s, :, pl.ds(to, n), :]
        return pltpu.make_async_remote_copy(
            src_ref=src, dst_ref=dst, send_sem=sx_sem.at[j, i], recv_sem=rx_sem.at[j, i],
            device_id=side_dev(dx, dy), device_id_type=MESH,
        )

    along_x = [i for i, (dx, dy) in enumerate(SIDES) if dy == 0]
    along_y = [i for i, (dx, dy) in enumerate(SIDES) if dx == 0]
    corners = [i for i, (dx, dy) in enumerate(SIDES) if dx and dy]

    def send(j, which):
        for i in which:
            pl.when(exists(*SIDES[i]))(lambda i=i: face(j, i).start())

    def sent(j):
        for i in range(8):
            pl.when(exists(*SIDES[i]))(lambda i=i: face(j, i).wait_send())
            if j == 0:
                pl.when(exists(*SIDES[i]))(lambda i=i: block_copy(i).wait_send())

    def receive(j):
        for i, (dx, dy) in enumerate(SIDES):
            pl.when(exists(-dx, -dy))(lambda i=i: face(j, i).wait_recv())

    for i in corners + along_x + along_y:
        pl.when(exists(*SIDES[i]))(lambda i=i: block_copy(i).start())
    send(0, along_x + corners + along_y)
    line_inverses(kpad[...], (w0, w1))

    def line_pass(j):
        def body(i, carry):
            for x8 in range(2 * ROWS):
                x = i * 2 * ROWS + x8
                e0 = split_mm(rhos[j][x + HALO].reshape(128, 128), w0[...])
                put(e0b, cb0, HALO, x, 0, e0[:NY2])
                put(e0b, cb0, HALO, x, 1, e0[NY2:])
            return carry

        lax.fori_loop(0, NXL // (2 * ROWS), body, 0)

    line_pass(0)

    for i in range(8):
        dx, dy = SIDES[i]
        pl.when(exists(-dx, -dy))(lambda i=i: block_copy(i).wait_recv())

    low_half = lax.broadcasted_iota(jnp.int32, (96, 128), 1) < 64

    def around(rows):
        def column(dy):
            parts = []
            for dx in (-1, 0, 1):
                if (dx, dy) == (0, 0):
                    parts.append(blk[rows, :])
                else:
                    parts.append(nbr[SIDES.index((-dx, -dy)), rows, :])
            return roll(jnp.concatenate(parts, axis=0), 64, 1)

        left, mid, right = column(-1), column(0), column(1)
        return jnp.concatenate(
            [jnp.where(low_half, left, mid), jnp.where(low_half, mid, right)], axis=1
        )

    def local(v):
        a, b = roll(v[:, 0:128], 64, 1), roll(v[:, 128:256], 64, 1)
        return jnp.where(low_half[: v.shape[0]], a, b)

    moves = ((-1, 0), (1, 0), (-1, 1), (1, 1))
    mask2 = around(pl.ds(0, NXL))
    m2[...] = mask2
    bars[0] = around(pl.ds(NXL, NXL))
    open_sides = jnp.zeros((96, 256), F32)
    for i, (s, axis) in enumerate(moves):
        beside = roll(mask2, s, axis)
        mn[i] = beside
        open_sides = open_sides + beside
    own2 = mask2 * (4.0 - open_sides)
    to_columns(local(mask2[24:72]))
    expand(m3, 6, 8, -6)
    expand(m3, 40, 42, -6)
    to_columns(local(own2[24:72]))
    expand(q3, 6, 42, -6)
    for a in range(2):
        for s, at in ((0, 63 - a), (1, 192 + a)):
            sm[s, a] = jnp.broadcast_to(mask2[24:72, at : at + 1], (48, 128))
            sq[s, a] = jnp.broadcast_to(own2[24:72, at : at + 1], (48, 128))

    xi = lax.broadcasted_iota(jnp.int32, (96, 256), 0) + (gx * NXL - 32)
    yi = lax.broadcasted_iota(jnp.int32, (96, 256), 1) + (gy * 128 - 64)
    inside = (xi >= 0) & (xi < nx * NXL) & (yi >= 0) & (yi < ny * 128)
    dom = jnp.where(inside, 1.0, 0.0)

    even_x = lax.rem(lax.broadcasted_iota(jnp.int32, (96, 256), 0), 2) == 0
    even_y = lax.rem(lax.broadcasted_iota(jnp.int32, (96, 256), 1), 2) == 0
    even_s = lax.rem(lax.broadcasted_iota(jnp.int32, (48, 128), 0), 2) == 0

    def flow(v):
        total = None
        for i, (s, axis) in enumerate(moves):
            term = mn[i] * (roll(v, s, axis) - v)
            total = term if total is None else total + term
        return total

    def mean_step(j):
        m = m2[...]
        e0 = bars[j] * (1.0 / 4.1)
        t = 4.0 * e0 + flow(e0)
        t1 = m * t
        t1 = t1 + jnp.where(even_x, roll(t1, -1, 0), roll(t1, 1, 0))
        t1 = t1 + jnp.where(even_y, roll(t1, -1, 1), roll(t1, 1, 1))
        e1 = t1 * (1.0 / 4.4)
        c = (0.8 / 4.4) * t1
        for _ in range(SWEEPS - 1):
            beside = (roll(c, 2, 0) + roll(c, -2, 0)) + (roll(c, 2, 1) + roll(c, -2, 1))
            c = dom * (c + 0.8 * (t1 - (4.4 * c - beside)) / 4.4)
        f = e1 + c
        rem = m * (t + flow(f) + (e1 - 0.25 * t1) - 0.1 * c)
        d = rem * (1.0 / 4.1)
        ybars[j] = e0 + m * f + d
        bars[j + 1] = m * (4.0 * d + flow(d))

    def insert(dst, src, shift, x):
        dst[x + shift, 1, 7:8, :] = src[0, pl.ds(x + 8, 1), :]
        dst[x + shift, 0, 72:73, :] = src[1, pl.ds(x + 8, 1), :]

    def stencil_rows(src, shift, x0, count, parts=HALVES, less=None):
        out = {}
        for y0, n in parts:
            held = {}

            def centre(x, b):
                if (x, b) not in held:
                    held[x, b] = src[x0 + x + shift, b, 8 + y0 : 8 + y0 + n, :]
                return held[x, b]

            for x in range(count):
                minus = None if less is None else less(x, y0, n)
                for b in range(2):
                    at = 7 + y0 if b == 0 else 9 + y0
                    beside = centre(x, 1 - b) + src[x0 + x + shift, 1 - b, at : at + n, :]
                    beside = beside + (centre(x - 1, b) + centre(x + 1, b))
                    if minus is not None:
                        beside = beside - minus
                    q = q3[x0 + x + 2, b, y0 : y0 + n, :]
                    m = m3[x0 + x + 2, b, y0 : y0 + n, :]
                    out[x, y0, b] = q * centre(x, b) + m * beside
        return out

    def strip_beside(v):
        return roll(v, 1, 0) + roll(v, -1, 0)

    def halo_lines(j):
        for x in (-3, -2, -1, 32, 33, 34):
            e0 = split_mm(rhos[j][x + HALO].reshape(128, 128), w0[...])
            put(e0b, cb0, HALO, x, 0, e0[:NY2])
            put(e0b, cb0, HALO, x, 1, e0[NY2:])
        se0[...] = split_mm(sr[j].reshape(288, 128), w0[...]).reshape(2, 3, 48, 128)

    def strip_correct():
        t1 = []
        for s in range(2):
            near, mid, far = se0[s, 0], se0[s, 1], se0[s, 2]
            t = sq[s, 0] * near + sm[s, 0] * (cb0[s] + mid + strip_beside(near))
            t = t + sq[s, 1] * mid + sm[s, 1] * (near + far + strip_beside(mid))
            t1.append(t + jnp.where(even_s, roll(t, -1, 0), roll(t, 1, 0)))
        t1 = jnp.concatenate(t1, axis=0)
        e1 = split_mm(t1, w1[...])
        h1 = 0.25 * t1 + 3.0 * e1
        for s in range(2):
            part = e1[48 * s : 48 * s + 48]
            for a in range(2):
                se[s, a] = se0[s, a] + sm[s, a] * part
            sd[s] = h1[48 * s : 48 * s + 48]

    def strip_smooth():
        rem = []
        for s in range(2):
            near, far = se[s, 0], se[s, 1]
            rem.append(sq[s, 0] * near + sm[s, 0] * (cb[s] + far + strip_beside(near) - sd[s]))
        sd[...] = split_mm(jnp.concatenate(rem, axis=0), w0[...]).reshape(2, 48, 128)

    def correct_block(first, count, parts):
        x0 = 2 * first
        t = stencil_rows(e0b, HALO, x0, 2 * count, parts)
        keys = [(k, y0, n) for y0, n in parts for k in range(count)]
        t1 = jnp.concatenate(
            [
                (t[2 * k, y0, 0] + t[2 * k, y0, 1]) + (t[2 * k + 1, y0, 0] + t[2 * k + 1, y0, 1])
                for k, y0, n in keys
            ],
            axis=0,
        )
        e1 = split_mm(t1, w1[...])
        h1 = 0.25 * t1 + 3.0 * e1
        at = 0
        for k, y0, n in keys:
            part = e1[at : at + n]
            h1s[first + k + 1, y0 : y0 + n, :] = h1[at : at + n]
            at += n
            for x in (2 * k, 2 * k + 1):
                for b in range(2):
                    m = m3[x0 + x + 2, b, y0 : y0 + n, :]
                    e0 = e0b[x0 + x + HALO, b, 8 + y0 : 8 + y0 + n, :]
                    put(eb, cb, HALO, x0 + x, b, e0 + m * part, y0)

    def correct_inner():
        correct_block(1, NXL // 2 - 2, INNER)

    def correct_outer():
        for x in range(-2, NXL + 2):
            insert(e0b, se0.at[:, 0], HALO, x)
        correct_block(-1, 2, HALVES)
        correct_block(NXL // 2 - 1, 2, HALVES)
        correct_block(1, 14, OUTER)

    def smooth_rows(x0, count, half):
        for x in range(count):
            insert(eb, se.at[:, 0], HALO, x0 + x)
        rem = stencil_rows(
            eb, HALO, x0, count, HALVES,
            lambda x, y0, n: h1s[half(x) + 1, y0 : y0 + n, :],
        )
        d = split_mm(jnp.concatenate(list(rem.values()), axis=0), w0[...])
        return [(key, d[n * 32 : n * 32 + 32]) for n, key in enumerate(rem)]

    def smooth_put(j, x, y0, b, d, acc):
        y = eb[x + HALO, b, 8 + y0 : 40 + y0, :] + d
        put(db, None, 1, x, b, d, y0)
        ys[j][x, b, y0 : y0 + 32, :] = y
        return acc + tile_sum(rhos[j][x + HALO, b, y0 : y0 + 32, :] * y)

    def smooth_edges(j, acc):
        for x0 in (-1, NXL - EDGE):
            for (x, y0, b), d in smooth_rows(x0, EDGE + 1, lambda x: (x0 + x) // 2):
                if 0 <= x0 + x < NXL:
                    acc = smooth_put(j, x0 + x, y0, b, d, acc)
                else:
                    put(db, None, 1, x0 + x, b, d, y0)
        return acc

    def smooth_part(j, i, acc):
        x0 = EDGE + i * MID
        for (x, y0, b), d in smooth_rows(
            x0, MID, lambda x: EDGE // 2 + i * (MID // 2) + x // 2
        ):
            acc = smooth_put(j, x0 + x, y0, b, d, acc)
        return acc

    def next_part(j, x0, count, acc):
        shift = HALO if j + 1 < ITERS else 0
        for x in range(count):
            insert(db, sd, 1, x0 + x)
        new = stencil_rows(db, 1, x0, count)
        for (x, y0, b), v in new.items():
            rhos[j + 1][x0 + x + shift, b, y0 : y0 + 32, :] = v
            acc = acc + tile_sum(v * ys[j][x0 + x, b, y0 : y0 + 32, :])
            if j + 1 < ITERS:
                put_sides(ss.at[j + 1], x0 + x, b, v, y0)
        return acc

    def smooth_and_next(j):
        zero = jnp.zeros((8, 128), F32)
        acc = smooth_edges(j, zero)
        acc_next = next_part(j, 0, HALO, zero)
        acc_next = next_part(j, NXL - HALO, HALO, acc_next)
        if j + 1 < ITERS:
            send(j + 1, along_x)
        nus[2 * j] = lax.fori_loop(0, (NXL - 2 * EDGE) // MID, lambda i, a: smooth_part(j, i, a), acc)
        inner = (NXL - 2 * HALO) // 2
        acc_next = lax.fori_loop(
            0, 2, lambda i, a: next_part(j, HALO + i * inner, inner, a), acc_next
        )
        if j + 1 < ITERS:
            send(j + 1, corners + along_y)
        nus[2 * j + 1] = acc_next

    dot_rows = lax.broadcasted_iota(jnp.int32, (8, 128), 0)
    here = pl.ds(32, NXL)

    def dot_row(n, v):
        return jnp.where(dot_rows == n, jnp.sum(v, axis=0, keepdims=True), 0.0)

    def mean_results():
        bar = [local(bars[n, here]) for n in range(ITERS + 1)]
        ybar = [local(ybars[n, here]) for n in range(ITERS)]
        part = dot_row(0, nu0)
        for n in range(2 * ITERS):
            v = 128.0 * tile_sum(bar[(n + 1) // 2] * ybar[n // 2])
            part = part + dot_row(n, v + nus[n] if n < 4 else v)
        dots[...] = part
        for n, v in enumerate(ybar + bar[1:]):
            to_columns(v)
            for b in range(2):
                cols[n, b] = tmat[pl.ds(b, NY2, stride=2), :]

    for j in range(ITERS):
        if j > 0:
            line_pass(j)
            sent(j - 1)
        correct_inner()
        if j == 1:
            mean_step(0)
            mean_step(1)
        if j == 2:
            mean_step(2)
            mean_results()
        receive(j)
        halo_lines(j)
        strip_correct()
        correct_outer()
        strip_smooth()
        smooth_and_next(j)

    part = dots[...]
    for n in (4, 5):
        part = part + dot_row(n, nus[n])
    total, copies = part, []
    for n, devs in enumerate(phases):
        red, base = reds[n], len(copies)
        red[0] = total
        for i, dev in enumerate(devs):
            copy = pltpu.make_async_remote_copy(
                src_ref=red.at[0], dst_ref=red.at[i + 1], send_sem=ss_sem.at[base + i],
                recv_sem=rs_sem.at[n], device_id=dev, device_id_type=MESH,
            )
            copy.start()
            copies.append(copy)
        if n == 1:
            sent(ITERS - 1)
            for copy in copies[:base]:
                copy.wait_send()
        rest = red.at[pl.ds(1, len(devs))]
        pltpu.make_async_copy(rest, rest, rs_sem.at[n]).wait()
        total = jnp.sum(red[...], axis=0)
    total = jnp.broadcast_to(jnp.sum(total, axis=1, keepdims=True), (8, 128))
    nu = [total[n : n + 1] for n in range(2 * ITERS)]

    h00, h10, h20 = nu[0] - nu[1], nu[1] - nu[2], nu[2] - nu[3]
    h11, h21, h22 = nu[2] - nu[3], nu[3] - nu[4], nu[4] - nu[5]
    l10, l20 = h10 / h00, h20 / h00
    d1, s21 = h11 - l10 * h10, h21 - l10 * h20
    l21 = s21 / d1
    d2 = h22 - l20 * h20 - l21 * s21
    b1 = nu[1] - l10 * nu[0]
    b2 = nu[2] - l20 * nu[0] - l21 * b1
    c2 = b2 / d2
    c1 = b1 / d1 - l21 * c2
    c0 = nu[0] / h00 - l10 * c1 - l20 * c2
    a0, a1, a2 = 1.0 - c0, c0 - c1, c1 - c2

    xcols = [c0 * cols[0, b] + c1 * cols[1, b] + c2 * cols[2, b] for b in range(2)]
    rcols = [a1 * cols[3, b] + a2 * cols[4, b] + c2 * cols[5, b] for b in range(2)]

    for g in range(4):
        for x in range(8 * g, 8 * g + 8):
            for b in range(2):
                v = inp[x, pl.ds(b, NY2, stride=2), :]
                m = m3[x + 2, b]
                ox = c0 * y0[x, b] + c1 * y1[x, b] + c2 * y2[x, b]
                ox = ox + c0 * ((1.0 - m) * v) + xcols[b][:, x : x + 1]
                orr = a0 * v + a1 * rho1[x + HALO, b] + a2 * rho2[x + HALO, b] + c2 * rho3[x, b]
                orr = orr + rcols[b][:, x : x + 1]
                x_ref[x, pl.ds(b, NY2, stride=2), :] = ox
                r_ref[x, pl.ds(b, NY2, stride=2), :] = orr

    for copy in copies[len(phases[0]):]:
        copy.wait_send()


def shards(nx, ny, right_side, sea_mask, vertical_coupling):
    vmem = pltpu.VMEM
    sizes = {"x": nx // 8, "y": 4, "c": 2, "z": ny}
    counts = [math.prod(sizes[axis] for axis in axes) for axes in PHASES]
    counts = counts + [1] * (3 - len(counts))
    out = pltpu.VMEM(right_side.shape, F32)
    return pl.pallas_call(
        functools.partial(kernel, nx, ny),
        out_shape=(out, out),
        in_specs=[
            pl.BlockSpec(memory_space=pltpu.HBM),
            pl.BlockSpec(memory_space=pltpu.HBM),
            pl.BlockSpec(memory_space=pltpu.HBM),
        ],
        out_specs=(pl.BlockSpec(memory_space=vmem), pl.BlockSpec(memory_space=vmem)),
        scratch_shapes=[
            vmem((NXL, 128), jnp.int32),
            vmem((1, 127), F32),
            vmem((NXL, 128, 128), F32),
            vmem((NXL + 2 * HALO, 2, NY2, 128), F32),
            vmem((NXL + 2 * HALO, 2, NY2, 128), F32),
            vmem((NXL + 2 * HALO, 2, NY2, 128), F32),
            vmem((NXL, 2, NY2, 128), F32),
            vmem((NXL, 2, NY2, 128), F32),
            vmem((NXL, 2, NY2, 128), F32),
            vmem((NXL, 2, NY2, 128), F32),
            vmem((NXL + 2 * HALO, 2, 80, 128), F32),
            vmem((NXL + 2 * HALO, 2, 80, 128), F32),
            vmem((NXL + 2, 2, 80, 128), F32),
            vmem((NXL // 2 + 2, NY2, 128), F32),
            vmem((NXL + 4, 2, NY2, 128), F32),
            vmem((NXL + 4, 2, NY2, 128), F32),
            vmem((ITERS, 2, 3, 48, 128), F32),
            vmem((ITERS, 2, 3, NXL, 128), F32),
            vmem((2, 3, 48, 128), F32),
            vmem((2, 2, 48, 128), F32),
            vmem((2, 48, 128), F32),
            vmem((2, 48, 128), F32),
            vmem((2, 48, 128), F32),
            vmem((2, 2, 48, 128), F32),
            vmem((2, 2, 48, 128), F32),
            vmem((256, 256), BF16),
            vmem((256, 256), BF16),
            vmem((1, 128), F32),
            vmem((2 * NXL, 128), F32),
            vmem((8, 2 * NXL, 128), F32),
            vmem((128, 128), F32),
            vmem((4, 96, 256), F32),
            vmem((96, 256), F32),
            vmem((ITERS + 1, 96, 256), F32),
            vmem((ITERS, 96, 256), F32),
            vmem((2 * ITERS, 8, 128), F32),
            vmem((8, 128), F32),
            vmem((2 * ITERS, 2, NY2, 128), F32),
            *[vmem((n, 8, 128), F32) for n in counts],
            pltpu.SemaphoreType.DMA((3,)),
            pltpu.SemaphoreType.DMA((ITERS, 8)),
            pltpu.SemaphoreType.DMA((ITERS, 8)),
            pltpu.SemaphoreType.DMA((8,)),
            pltpu.SemaphoreType.DMA((8,)),
            pltpu.SemaphoreType.DMA((sum(counts),)),
            pltpu.SemaphoreType.DMA((2,)),
        ],
        compiler_params=pltpu.CompilerParams(
            collective_id=0, has_side_effects=True, vmem_limit_bytes=56 * 1024 * 1024
        ),
    )(right_side, sea_mask, vertical_coupling.reshape(1, -1))


def solution(mesh):
    nx, ny = mesh.shape["gx"], mesh.shape["gy"]
    return jax.shard_map(
        functools.partial(shards, nx, ny),
        mesh=mesh,
        in_specs=(P("gx", "gy", None), P("gx", "gy"), P()),
        out_specs=(P("gx", "gy", None), P("gx", "gy", None)),
        check_vma=False,
    )
```
